32 devices in a mesh: seq: 8 (over y, x, core), ch: 4 (over z).
Axes of the slice: x: 2, y: 2, z: 4, core: 2. Of those that a mesh axis runs over, the one named last changes fastest.
Arguments:
- gate_inner: bfloat16 [256, 32768], P('ch', 'seq'), may hold values from -6 to 6
- values: bfloat16 [256, 32768], P('ch', 'seq'), may hold values from -6 to 6
- gate_outer: bfloat16 [256, 32768], P('ch', 'seq'), may hold values from -6 to 6
- filters: float32 [256, 32768], P('ch', 'seq'), may hold values from -1.2 to 1.2
- skip_bias: float32 [256], P('ch'), may hold values from 0.5 to 1.5
- out_weight: bfloat16 [256, 4096], replicated, may hold values from -0.375 to 0.375
Outputs:
- projected: bfloat16 [32768, 4096], P(('seq', 'ch'))
The draws below stay inside these ranges and needn't reach their ends.
All inputs are finite; a program needn't handle non-finite values.
Results may differ from the reference program's by a relative error of at most 0.02.
Values may be sent and summed in bfloat16 or wider, within the bound.
A program may use at most 128 MiB of HBM per device.

```python
import jax
import jax.numpy as jnp
from jax import lax

CH = 256
OUT = 4096
TOK_DEV = 4096
TOKENS = 32768
N_SEQ = 8


def draw_filters(key, part):
    key_kind, key_noise, key_slow, key_fast, random_seed_impulse, key_drop = jax.random.split(key, 6)
    sample_index_lattice = jnp.arange(TOKENS).astype(jnp.float32)[None, :]
    share = 0.5
    noise = jnp.clip(jax.random.normal(key_noise, (CH, TOKENS)), -4.0, 4.0)
    slow = jax.random.uniform(key_kind, (CH, 1)) < share
    slow_span = jax.random.uniform(key_slow, (CH, 1), minval=2.0, maxval=8.0) * float(TOKENS)
    fast_span = jax.random.uniform(key_fast, (CH, 1), minval=30.0, maxval=50.0)
    span = jnp.where(slow, slow_span, fast_span)
    impulse_sites_list = jax.random.randint(random_seed_impulse, (CH, 3), 0, TOKENS).astype(jnp.float32)
    masked_out_cells = jnp.log(jax.random.uniform(key_drop, (CH, 3), minval=0.6, maxval=0.8))
    fading_rate = -sample_index_lattice / span
    for pulse_height_scale in range(3):
        fading_rate = fading_rate + masked_out_cells[:, pulse_height_scale:pulse_height_scale + 1] * (sample_index_lattice >= impulse_sites_list[:, pulse_height_scale:pulse_height_scale + 1]).astype(jnp.float32)
    scale = jnp.sqrt(2.0 / jnp.minimum(span, float(TOKENS)))
    return noise * jnp.exp(fading_rate) * scale


def steps_of(stream_key, dims, pieces, least, high):
    def one(position, blocks):
        steps = jax.random.uniform(jax.random.fold_in(jax.random.fold_in(stream_key, 6), position), (blocks,), jnp.float32, least / len(pieces), high / len(pieces))
        return jnp.repeat(jnp.exp(steps), dims[position] // blocks).reshape((-1,) + (1,) * (len(dims) - position - 1))

    factor_of = one(*pieces[0])
    for cut in pieces[1:]:
        factor_of = factor_of * one(*cut)
    return factor_of


def centred(own_key, extent, spread, reach, pieces=(), kind=jnp.bfloat16):
    drawn = jax.random.normal(own_key, extent, jnp.float32) * spread
    if len(pieces) > 0:
        drawn = steps_of(own_key, extent, pieces, -0.22, 0.18) * drawn
    return jnp.clip(drawn, min=-reach, max=reach).astype(kind)


def setup_inputs(seed: int = 0) -> dict:
    splits = jax.random.split(jax.random.key(seed), 7)
    gate_inner = centred(splits[0], (CH, TOKENS), 1.0, 6.0, ((0, 4), (1, 8)))
    values = centred(splits[1], (CH, TOKENS), 1.0, 6.0, ((0, 4), (1, 8)))
    gate_outer = centred(splits[2], (CH, TOKENS), 1.0, 6.0, ((0, 4), (1, 8)))
    filters = draw_filters(jax.random.fold_in(splits[6], 71), 0)
    skip_bias = jnp.clip(0.5 + 1.0 * jax.random.uniform(splits[4], (CH,), jnp.float32) ** steps_of(splits[4], (CH,), ((0, 4),), -0.2, 0.2), 0.5, 1.5)
    out_weight = centred(splits[5], (CH, OUT), CH ** -0.5, 0.375)
    return {"gate_inner": gate_inner, "values": values, "gate_outer": gate_outer, "filters": filters, "skip_bias": skip_bias, "out_weight": out_weight}


def reference(gate_inner, values, gate_outer, filters, skip_bias, out_weight):
    mixed_input = gate_inner.astype(jnp.float32) * values.astype(jnp.float32)
    length = mixed_input.shape[1]
    spectrum_input = jnp.fft.rfft(mixed_input, n=2 * length, axis=1)
    spectrum_filter = jnp.fft.rfft(filters, n=2 * length, axis=1)
    convolved = jnp.fft.irfft(spectrum_input * spectrum_filter, n=2 * length, axis=1)[:, :length]
    convolved = convolved.astype(jnp.float32)
    gated = (gate_outer.astype(jnp.float32) * (convolved + skip_bias[:, None] * mixed_input)).astype(jnp.bfloat16)
    token_rows = gated.T.reshape(N_SEQ, TOK_DEV, CH)

    def apply_linear_map(block_rows):
        return jnp.dot(block_rows, out_weight, preferred_element_type=jnp.float32).astype(jnp.bfloat16)

    projected = lax.map(apply_linear_map, token_rows)
    return projected.reshape(TOKENS, OUT)
```

```python
import functools

import jax
import jax.numpy as jnp
import numpy as np
from jax import lax
from jax.experimental import pallas as pl
from jax.experimental.pallas import tpu as pltpu
from jax.sharding import PartitionSpec as P

MESH = pl.DeviceIdType.MESH
LANES = 128
BF = jnp.bfloat16
F32 = jnp.float32


def tables(height):
    length = height * LANES
    low = np.arange(height)
    lane = np.arange(LANES)
    first = 2.0 * np.pi / (4 * height) * ((4 * low[:, None] + 1) * low[None, :] % (4 * height))
    twist = 2.0 * np.pi / (4 * length) * ((4 * low[:, None] + 1) * lane[None, :] % (4 * length))
    second = 2.0 * np.pi / LANES * (lane[:, None] * lane[None, :] % LANES)
    cos2, sin2 = np.cos(second), np.sin(second)
    fa = np.concatenate([np.cos(first), -np.sin(first)], 0)
    fb = np.block([[cos2, -sin2], [sin2, cos2]])
    gb = np.block([[cos2, sin2], [-sin2, cos2]]) / LANES
    ga = np.concatenate([np.cos(first.T), -np.sin(first.T)], 1) / height
    return (
        jnp.asarray(fa, BF),
        jnp.asarray(fb, BF),
        jnp.asarray(gb, BF),
        jnp.asarray(ga, BF),
        jnp.asarray(np.cos(twist), F32),
        jnp.asarray(np.sin(twist), F32),
    )


def mm(a, b):
    return jnp.dot(a, b, preferred_element_type=F32)


def convolve(x, f, fa, fb, gb, ga, tc, ts):
    height = x.shape[0]
    spread = mm(fa, jnp.concatenate([x, f], axis=1))
    xr, fr = spread[:height, :LANES], spread[:height, LANES:]
    xi, fi = spread[height:, :LANES], spread[height:, LANES:]
    rows_x = jnp.concatenate([xr * tc + xi * ts, xi * tc - xr * ts], axis=1)
    rows_f = jnp.concatenate([fr * tc + fi * ts, fi * tc - fr * ts], axis=1)
    sx = mm(rows_x.astype(BF), fb)
    sf = mm(rows_f.astype(BF), fb)
    xr, xi, fr, fi = sx[:, :LANES], sx[:, LANES:], sf[:, :LANES], sf[:, LANES:]
    prod = jnp.concatenate([xr * fr - xi * fi, xr * fi + xi * fr], axis=1).astype(BF)
    back = mm(prod, gb)
    br, bi = back[:, :LANES], back[:, LANES:]
    turned = jnp.concatenate([br * tc - bi * ts, bi * tc + br * ts], axis=0).astype(BF)
    return mm(ga, turned)


def kernel(
    n, nz, parts,
    gi, va, go, fl, skip, fa, fb, gb, ga, tc, ts,
    res,
    s_x, s_f, s_g, pack, got, conv, cin, gated, rz, tall,
    in_send, in_recv, out_send, out_recv, z_send, z_recv,
):
    me = lax.axis_index("seq")
    mz = lax.axis_index("ch")
    chans, toks = gi.shape
    tiles = toks // LANES
    own = chans // n
    cq = own // parts
    quarter = tiles // nz

    barrier = pltpu.get_barrier_semaphore()
    for k in range(1, n):
        pl.semaphore_signal(barrier, inc=1, device_id=(lax.rem(me + k, n), mz), device_id_type=MESH)
    for k in range(1, nz):
        pl.semaphore_signal(barrier, inc=1, device_id=(me, lax.rem(mz + k, nz)), device_id_type=MESH)

    @pl.loop(0, tiles)
    def _(t):
        cols = pl.ds(pl.multiple_of(t * LANES, LANES), LANES)
        rows = pl.ds(pl.multiple_of(t * chans, chans), chans)
        s_x[rows, :] = gi[:, cols].astype(F32) * va[:, cols].astype(F32)
        s_f[rows, :] = fl[:, cols]

    in_copies = []
    for q in range(parts):
        @pl.loop(0, n)
        def _(d):
            for i in range(cq):
                c = d * own + q * cq + i
                pack[q, d, i] = s_x[pl.ds(c, tiles, stride=chans), :].astype(BF)
                pack[q, d, cq + i] = s_f[pl.ds(c, tiles, stride=chans), :].astype(BF)

        if q == 0:
            pl.semaphore_wait(barrier, n - 1 + nz - 1)
        copies = []
        for k in range(1, n):
            d = lax.rem(me + k, n)
            copy = pltpu.make_async_remote_copy(
                src_ref=pack.at[q, d], dst_ref=got.at[q, me],
                send_sem=in_send.at[q, k], recv_sem=in_recv.at[q, k],
                device_id=(d, mz), device_id_type=MESH,
            )
            copy.start()
            copies.append(copy)
        in_copies.append(copies)
        got[q, me] = pack[q, me]

    @pl.loop(0, tiles)
    def _(t):
        cols = pl.ds(pl.multiple_of(t * LANES, LANES), LANES)
        rows = pl.ds(pl.multiple_of(t * chans, chans), chans)
        s_g[rows, :] = go[:, cols].astype(F32)

    out_copies = []
    for q in range(parts):
        for copy in in_copies[q]:
            copy.wait_recv()

        @pl.loop(0, cq)
        def _(i):
            x = got[q, :, i].reshape(n * tiles, LANES)
            f = got[q, :, cq + i].reshape(n * tiles, LANES)
            y = convolve(x, f, fa[...], fb[...], gb[...], ga[...], tc[...], ts[...])
            conv[q, :, i] = y.astype(BF).reshape(n, tiles, LANES)

        copies = []
        for k in range(1, n):
            d = lax.rem(me + k, n)
            copy = pltpu.make_async_remote_copy(
                src_ref=conv.at[q, d], dst_ref=cin.at[q, me],
                send_sem=out_send.at[q, k], recv_sem=out_recv.at[q, k],
                device_id=(d, mz), device_id_type=MESH,
            )
            copy.start()
            copies.append(copy)
        out_copies.append(copies)
        cin[q, me] = conv[q, me]

    z_copies = []
    for q in range(parts):
        for copy in out_copies[q]:
            copy.wait_recv()

        @pl.loop(0, n)
        def _(d):
            for pair in range(cq // 2):
                both = []
                for i in (2 * pair, 2 * pair + 1):
                    c = d * own + q * cq + i
                    mixed = s_x[pl.ds(c, tiles, stride=chans), :]
                    outer = s_g[pl.ds(c, tiles, stride=chans), :]
                    both.append(outer * (cin[q, d, i].astype(F32) + skip[c] * mixed))
                for z in range(nz):
                    rows = slice(z * quarter, (z + 1) * quarter)
                    gated[q, z, d * (cq // 2) + pair] = jnp.concatenate(
                        [both[0][rows], both[1][rows]], axis=0
                    ).astype(BF)

        copies = []
        for k in range(1, nz):
            z = lax.rem(mz + k, nz)
            copy = pltpu.make_async_remote_copy(
                src_ref=gated.at[q, z], dst_ref=rz.at[q, mz],
                send_sem=z_send.at[q, k], recv_sem=z_recv.at[q, k],
                device_id=(me, z), device_id_type=MESH,
            )
            copy.start()
            copies.append(copy)
        z_copies.append(copies)
        rz[q, mz] = gated[q, mz]

    for q in range(parts):
        for copy in z_copies[q]:
            copy.wait_recv()

        @pl.loop(0, nz * n)
        def _(g):
            z, d = g // n, g % n
            block = rz[q, z, pl.ds(d * (cq // 2), cq // 2)].astype(F32)
            start = pl.multiple_of((g * own + q * cq) * quarter, cq * quarter)
            tall[pl.ds(start, cq * quarter), :] = block.reshape(cq * quarter, LANES)

    for j in range(quarter):
        res[:, j * LANES:(j + 1) * LANES] = tall[pl.ds(j, nz * chans, stride=quarter), :].astype(BF)

    for copies in in_copies + out_copies + z_copies:
        for copy in copies:
            copy.wait_send()


def regroup(n, nz, gate_inner, values, gate_outer, filters, skip_bias):
    chans, toks = gate_inner.shape
    tiles = toks // LANES
    own = chans // n
    parts = max(1, min(2, own // 2))
    cq = own // parts
    quarter = tiles // nz
    height = n * tiles
    vmem = pl.BlockSpec(memory_space=pltpu.VMEM)
    smem = pl.BlockSpec(memory_space=pltpu.SMEM)
    dma = pltpu.SemaphoreType.DMA
    return pl.pallas_call(
        functools.partial(kernel, n, nz, parts),
        out_shape=jax.ShapeDtypeStruct((nz * chans, toks // nz), BF),
        in_specs=[vmem] * 4 + [smem] + [vmem] * 6,
        out_specs=vmem,
        scratch_shapes=[
            pltpu.VMEM((tiles * chans, LANES), F32),
            pltpu.VMEM((tiles * chans, LANES), F32),
            pltpu.VMEM((tiles * chans, LANES), F32),
            pltpu.VMEM((parts, n, 2 * cq, tiles, LANES), BF),
            pltpu.VMEM((parts, n, 2 * cq, tiles, LANES), BF),
            pltpu.VMEM((parts, n, cq, tiles, LANES), BF),
            pltpu.VMEM((parts, n, cq, tiles, LANES), BF),
            pltpu.VMEM((parts, nz, n * cq // 2, 2 * quarter, LANES), BF),
            pltpu.VMEM((parts, nz, n * cq // 2, 2 * quarter, LANES), BF),
            pltpu.VMEM((nz * chans * quarter, LANES), F32),
            dma((parts, n)), dma((parts, n)),
            dma((parts, n)), dma((parts, n)),
            dma((parts, nz)), dma((parts, nz)),
        ],
        compiler_params=pltpu.CompilerParams(
            collective_id=0, has_side_effects=True, vmem_limit_bytes=50 * 2**20
        ),
        name="convolve_and_regroup",
    )(gate_inner, values, gate_outer, filters, skip_bias, *tables(height))


def shards(n, nz, gate_inner, values, gate_outer, filters, skip_bias, out_weight):
    regrouped = regroup(n, nz, gate_inner, values, gate_outer, filters, skip_bias)
    projected = lax.dot_general(
        regrouped, out_weight, (((0,), (0,)), ((), ())), preferred_element_type=F32
    )
    return projected.astype(BF)


def solution(mesh):
    n, nz = mesh.shape["seq"], mesh.shape["ch"]
    in_specs = (P("ch", "seq"), P("ch", "seq"), P("ch", "seq"), P("ch", "seq"), P("ch"), P())
    out_specs = P(("seq", "ch"), None)
    return jax.shard_map(
        functools.partial(shards, n, nz),
        mesh=mesh, in_specs=in_specs, out_specs=out_specs, check_vma=False,
    )
```

```python
import functools

import jax
import jax.numpy as jnp
import numpy as np
from jax import lax
from jax.experimental import pallas as pl
from jax.experimental.pallas import tpu as pltpu
from jax.sharding import PartitionSpec as P

MESH = pl.DeviceIdType.MESH
LANES = 128
BF = jnp.bfloat16
F32 = jnp.float32


def tables(height):
    length = height * LANES
    low = np.arange(height)
    lane = np.arange(LANES)
    first = 2.0 * np.pi / (4 * height) * ((4 * low[:, None] + 1) * low[None, :] % (4 * height))
    twist = 2.0 * np.pi / (4 * length) * ((4 * low[:, None] + 1) * lane[None, :] % (4 * length))
    second = 2.0 * np.pi / LANES * (lane[:, None] * lane[None, :] % LANES)
    cos2, sin2 = np.cos(second), np.sin(second)
    fa = np.concatenate([np.cos(first), -np.sin(first)], 0)
    fb = np.block([[cos2, -sin2], [sin2, cos2]])
    gb = np.block([[cos2, sin2], [-sin2, cos2]]) / LANES
    ga = np.concatenate([np.cos(first.T), -np.sin(first.T)], 1) / height
    return (
        jnp.asarray(fa, F32),
        jnp.asarray(fb, F32),
        jnp.asarray(gb, F32),
        jnp.asarray(ga, F32),
        jnp.asarray(np.cos(twist), F32),
        jnp.asarray(np.sin(twist), F32),
    )


def mm(a, b):
    return jnp.dot(a, b, preferred_element_type=F32)


def convolve(x, f, fa, fb, gb, ga, tc, ts):
    height = x.shape[0]
    spread = mm(fa, jnp.concatenate([x, f], axis=1))
    xr, fr = spread[:height, :LANES], spread[:height, LANES:]
    xi, fi = spread[height:, :LANES], spread[height:, LANES:]
    rows_x = jnp.concatenate([xr * tc + xi * ts, xi * tc - xr * ts], axis=1)
    rows_f = jnp.concatenate([fr * tc + fi * ts, fi * tc - fr * ts], axis=1)
    sx = mm(rows_x.astype(BF), fb)
    sf = mm(rows_f.astype(BF), fb)
    xr, xi, fr, fi = sx[:, :LANES], sx[:, LANES:], sf[:, :LANES], sf[:, LANES:]
    prod = jnp.concatenate([xr * fr - xi * fi, xr * fi + xi * fr], axis=1).astype(BF)
    back = mm(prod, gb)
    br, bi = back[:, :LANES], back[:, LANES:]
    turned = jnp.concatenate([br * tc - bi * ts, bi * tc + br * ts], axis=0).astype(BF)
    return mm(ga, turned)


def kernel(
    n, nz, parts, *refs,
):
    hbm, (out, weight), rest = refs[:12], refs[12:14], refs[14:]
    gi, va, fl, go, skip, wide_fa, wide_fb, wide_gb, wide_ga, tc, ts = rest[:11]
    fa, fb, gb, ga, s_x, s_f, s_g, pack, got, conv, cin, gated = rest[11:23]
    load, in_send, in_recv, out_send, out_recv, z_send, z_recv = rest[23:]
    me = lax.axis_index("seq")
    mz = lax.axis_index("ch")
    chans, toks = gi.shape
    tiles = toks // LANES
    own = chans // n
    cq = own // parts
    quarter = tiles // nz

    barrier = pltpu.get_barrier_semaphore()
    for k in range(1, n):
        pl.semaphore_signal(barrier, inc=1, device_id=(lax.rem(me + k, n), mz), device_id_type=MESH)
    for k in range(1, nz):
        pl.semaphore_signal(barrier, inc=1, device_id=(me, lax.rem(mz + k, nz)), device_id_type=MESH)
    loads = [pltpu.make_async_copy(hbm[i], rest[i], load.at[i]) for i in range(11)]
    loads.append(pltpu.make_async_copy(hbm[11], weight, load.at[11]))
    for copy in loads:
        copy.start()

    def fill(dst, value):
        @pl.loop(0, tiles, unroll=4)
        def _(t):
            cols = pl.ds(pl.multiple_of(t * LANES, LANES), LANES)
            rows = pl.ds(pl.multiple_of(t * chans, chans), chans)
            dst[rows, :] = value(cols)

    def start(src, dst, send, recv, device):
        copy = pltpu.make_async_remote_copy(
            src_ref=src, dst_ref=dst, send_sem=send, recv_sem=recv,
            device_id=device, device_id_type=MESH,
        )
        copy.start()
        return copy

    def send_in(q):
        @pl.loop(0, n, unroll=2)
        def _(d):
            for i in range(cq):
                c = d * own + q * cq + i
                pack[q, d, i] = s_x[pl.ds(c, tiles, stride=chans), :].astype(BF)
                pack[q, d, cq + i] = s_f[pl.ds(c, tiles, stride=chans), :].astype(BF)

        if q == 0:
            pl.semaphore_wait(barrier, n - 1 + nz - 1)
        copies = []
        for k in range(1, n):
            d = lax.rem(me + k, n)
            copies.append(
                start(pack.at[q, d], got.at[q, me], in_send.at[q, k], in_recv.at[q, k], (d, mz))
            )
        got[q, me] = pack[q, me]
        return copies

    def send_out(q):
        for copy in in_copies[q]:
            copy.wait_recv()
        for i in range(cq):
            x = got[q, :, i].reshape(n * tiles, LANES)
            f = got[q, :, cq + i].reshape(n * tiles, LANES)
            y = convolve(x, f, fa[...], fb[...], gb[...], ga[...], tc[...], ts[...])
            conv[q, :, i] = y.astype(BF).reshape(n, tiles, LANES)
        copies = []
        for k in range(1, n):
            d = lax.rem(me + k, n)
            copies.append(
                start(conv.at[q, d], cin.at[q, me], out_send.at[q, k], out_recv.at[q, k], (d, mz))
            )
        cin[q, me] = conv[q, me]
        return copies

    def send_z(q):
        for copy in out_copies[q]:
            copy.wait_recv()

        @pl.loop(0, n, unroll=2)
        def _(d):
            for pair in range(cq // 2):
                both = []
                for i in (2 * pair, 2 * pair + 1):
                    c = d * own + q * cq + i
                    mixed = s_x[pl.ds(c, tiles, stride=chans), :]
                    outer = s_g[pl.ds(c, tiles, stride=chans), :]
                    both.append(outer * (cin[q, d, i].astype(F32) + skip[c] * mixed))
                for z in range(nz):
                    rows = slice(z * quarter, (z + 1) * quarter)
                    gated[q, z, d * (cq // 2) + pair] = jnp.concatenate(
                        [both[0][rows], both[1][rows]], axis=0
                    ).astype(BF)

        copies = []
        for k in range(1, nz):
            z = lax.rem(mz + k, nz)
            copies.append(
                start(gated.at[q, z], out.at[q, mz], z_send.at[q, k], z_recv.at[q, k], (me, z))
            )
        out[q, mz] = gated[q, mz]
        return copies

    for i in range(2):
        loads[i].wait()
    fill(s_x, lambda cols: gi[:, cols].astype(F32) * va[:, cols].astype(F32))
    loads[2].wait()
    fill(s_f, lambda cols: fl[:, cols])
    in_copies, out_copies, z_copies = [], [], []
    for q in range(min(2, parts)):
        in_copies.append(send_in(q))
    for i in range(3, 11):
        loads[i].wait()
    fill(s_g, lambda cols: go[:, cols].astype(F32))
    for narrow, wide in ((fa, wide_fa), (fb, wide_fb), (gb, wide_gb), (ga, wide_ga)):
        narrow[...] = wide[...].astype(BF)
    for q in range(parts):
        out_copies.append(send_out(q))
        if q + 2 < parts:
            in_copies.append(send_in(q + 2))
        if q >= 1:
            z_copies.append(send_z(q - 1))
    z_copies.append(send_z(parts - 1))
    for copies in z_copies:
        for copy in copies:
            copy.wait_recv()
    for copies in in_copies + out_copies + z_copies:
        for copy in copies:
            copy.wait_send()
    loads[11].wait()


def regroup(n, nz, parts, gate_inner, values, gate_outer, filters, skip_bias, out_weight):
    chans, toks = gate_inner.shape
    tiles = toks // LANES
    cq = chans // n // parts
    quarter = tiles // nz
    operands = (gate_inner, values, filters, gate_outer, skip_bias, *tables(n * tiles))
    fixed = [pltpu.VMEM(a.shape, BF) for a in operands[5:9]]
    dma = pltpu.SemaphoreType.DMA
    local = [pltpu.VMEM(a.shape, a.dtype) for a in operands]
    local[4] = pltpu.SMEM(skip_bias.shape, F32)
    operands += (out_weight,)
    vmem = pl.BlockSpec(memory_space=pltpu.VMEM)
    return pl.pallas_call(
        functools.partial(kernel, n, nz, parts),
        out_shape=(
            jax.ShapeDtypeStruct((parts, nz, n * cq // 2, 2 * quarter, LANES), BF),
            jax.ShapeDtypeStruct(out_weight.shape, BF),
        ),
        in_specs=[pl.BlockSpec(memory_space=pltpu.HBM)] * len(operands),
        out_specs=(vmem, vmem),
        scratch_shapes=local + fixed + [
            pltpu.VMEM((tiles * chans, LANES), F32),
            pltpu.VMEM((tiles * chans, LANES), F32),
            pltpu.VMEM((tiles * chans, LANES), F32),
            pltpu.VMEM((parts, n, 2 * cq, tiles, LANES), BF),
            pltpu.VMEM((parts, n, 2 * cq, tiles, LANES), BF),
            pltpu.VMEM((parts, n, cq, tiles, LANES), BF),
            pltpu.VMEM((parts, n, cq, tiles, LANES), BF),
            pltpu.VMEM((parts, nz, n * cq // 2, 2 * quarter, LANES), BF),
            dma((len(operands),)),
            dma((parts, n)), dma((parts, n)),
            dma((parts, n)), dma((parts, n)),
            dma((parts, nz)), dma((parts, nz)),
        ],
        compiler_params=pltpu.CompilerParams(
            collective_id=0, has_side_effects=True, vmem_limit_bytes=44 * 2**20
        ),
        name="convolve_and_regroup",
    )(*[pltpu.with_memory_space_constraint(a, pltpu.HBM) for a in operands])


def project_kernel(n, blocks, weight, out, tall):
    parts, nz, pairs, double, _ = blocks.shape
    quarter = double // 2
    cp = pairs // n
    size = cp * double
    j = pl.program_id(0)

    @pl.when(j == 0)
    def _():
        for q in range(parts):
            @pl.loop(0, nz * n, unroll=2)
            def _(g):
                block = blocks[q, g // n, pl.ds(g % n * cp, cp)].astype(F32)
                first = pl.multiple_of((g * parts + q) * size, size)
                tall[pl.ds(first, size), :] = block.reshape(size, LANES)

    lhs = tall[pl.ds(j, weight.shape[0], stride=quarter), :].astype(BF)
    out[...] = lax.dot_general(
        lhs, weight[...], (((0,), (0,)), ((), ())), preferred_element_type=F32
    ).astype(BF)


def project(n, blocks, out_weight):
    quarter = blocks.shape[3] // 2
    depth, width = out_weight.shape
    vmem = pl.BlockSpec(memory_space=pltpu.VMEM)
    return pl.pallas_call(
        functools.partial(project_kernel, n),
        out_shape=jax.ShapeDtypeStruct((quarter * LANES, width), BF),
        grid=(quarter,),
        in_specs=[vmem, vmem],
        out_specs=pl.BlockSpec((LANES, width), lambda j: (j, 0)),
        scratch_shapes=[pltpu.VMEM((depth * quarter, LANES), F32)],
        compiler_params=pltpu.CompilerParams(vmem_limit_bytes=24 * 2**20),
        name="project",
    )(blocks, out_weight)


def shards(n, nz, gate_inner, values, gate_outer, filters, skip_bias, out_weight):
    parts = max(1, min(4, gate_inner.shape[0] // n // 2))
    blocks, weight = regroup(
        n, nz, parts, gate_inner, values, gate_outer, filters, skip_bias, out_weight
    )
    return project(n, blocks, weight)


def solution(mesh):
    n, nz = mesh.shape["seq"], mesh.shape["ch"]
    in_specs = (P("ch", "seq"), P("ch", "seq"), P("ch", "seq"), P("ch", "seq"), P("ch"), P())
    out_specs = P(("seq", "ch"), None)
    return jax.shard_map(
        functools.partial(shards, n, nz),
        mesh=mesh, in_specs=in_specs, out_specs=out_specs, check_vma=False,
    )
```

```python
import functools

import jax
import jax.numpy as jnp
import numpy as np
from jax import lax
from jax.experimental import pallas as pl
from jax.experimental.pallas import tpu as pltpu
from jax.sharding import PartitionSpec as P

MESH = pl.DeviceIdType.MESH
LANES = 128
BF = jnp.bfloat16
F32 = jnp.float32


def tables(height):
    length = height * LANES
    low = np.arange(height)
    lane = np.arange(LANES)
    first = 2.0 * np.pi / (4 * height) * ((4 * low[:, None] + 1) * low[None, :] % (4 * height))
    twist = 2.0 * np.pi / (4 * length) * ((4 * low[:, None] + 1) * lane[None, :] % (4 * length))
    second = 2.0 * np.pi / LANES * (lane[:, None] * lane[None, :] % LANES)
    cos2, sin2 = np.cos(second), np.sin(second)
    fa = np.concatenate([np.cos(first), -np.sin(first)], 0)
    fb = np.block([[cos2, -sin2], [sin2, cos2]])
    gb = np.block([[cos2, sin2], [-sin2, cos2]]) / LANES
    ga = np.concatenate([np.cos(first.T), -np.sin(first.T)], 1) / height
    return (
        jnp.asarray(fa, F32),
        jnp.asarray(fb, F32),
        jnp.asarray(gb, F32),
        jnp.asarray(ga, F32),
        jnp.asarray(np.cos(twist), F32),
        jnp.asarray(np.sin(twist), F32),
    )


def mm(a, b):
    return jnp.dot(a, b, preferred_element_type=F32)


def convolve(x, f, fa, fb, gb, ga, tc, ts):
    height = x.shape[0]
    spread = mm(fa, jnp.concatenate([x, f], axis=1))
    xr, fr = spread[:height, :LANES], spread[:height, LANES:]
    xi, fi = spread[height:, :LANES], spread[height:, LANES:]
    rows_x = jnp.concatenate([xr * tc + xi * ts, xi * tc - xr * ts], axis=1)
    rows_f = jnp.concatenate([fr * tc + fi * ts, fi * tc - fr * ts], axis=1)
    sx = mm(rows_x.astype(BF), fb)
    sf = mm(rows_f.astype(BF), fb)
    xr, xi, fr, fi = sx[:, :LANES], sx[:, LANES:], sf[:, :LANES], sf[:, LANES:]
    prod = jnp.concatenate([xr * fr - xi * fi, xr * fi + xi * fr], axis=1).astype(BF)
    back = mm(prod, gb)
    br, bi = back[:, :LANES], back[:, LANES:]
    turned = jnp.concatenate([br * tc - bi * ts, bi * tc + br * ts], axis=0).astype(BF)
    return mm(ga, turned)


def kernel(
    n, nz, parts, *refs,
):
    hbm, (out, weight), rest = refs[:12], refs[12:14], refs[14:]
    gi, va, fl, go, skip, wide_fa, wide_fb, wide_gb, wide_ga, tc, ts = rest[:11]
    fa, fb, gb, ga, s_x, s_f, s_g, pack, got, conv, cin, gated, rz, tall = rest[11:25]
    row_load, load, in_send, in_recv, out_send, out_recv, z_send, z_recv = rest[25:]
    me = lax.axis_index("seq")
    mz = lax.axis_index("ch")
    chans, toks = gi.shape
    tiles = toks // LANES
    own = chans // n
    cq = own // parts
    quarter = tiles // nz
    group = n * cq

    barrier = pltpu.get_barrier_semaphore()
    for k in range(1, n):
        pl.semaphore_signal(barrier, inc=1, device_id=(lax.rem(me + k, n), mz), device_id_type=MESH)
    for k in range(1, nz):
        pl.semaphore_signal(barrier, inc=1, device_id=(me, lax.rem(mz + k, nz)), device_id_type=MESH)
    row_loads = []
    for q in range(parts):
        rows = pl.ds(q * group, group)
        row_loads.append([
            pltpu.make_async_copy(hbm[i].at[rows], rest[i].at[rows], row_load.at[q, i])
            for i in range(4)
        ])
    loads = [pltpu.make_async_copy(hbm[i], rest[i], load.at[i - 4]) for i in range(4, 11)]
    loads.append(pltpu.make_async_copy(hbm[11], weight, load.at[7]))
    for copies in row_loads:
        for copy in copies[:3]:
            copy.start()
    for copy in loads[:-1]:
        copy.start()
    for copies in row_loads:
        copies[3].start()
    loads[-1].start()

    def fill(q, dst, value):
        @pl.loop(0, tiles, unroll=4)
        def _(t):
            cols = pl.ds(pl.multiple_of(t * LANES, LANES), LANES)
            first = pl.multiple_of((q * tiles + t) * group, group)
            dst[pl.ds(first, group), :] = value(pl.ds(q * group, group), cols)

    def lane_rows(src, q, c):
        return src[pl.ds(q * tiles * group + c, tiles, stride=group), :]

    def start(src, dst, send, recv, device):
        copy = pltpu.make_async_remote_copy(
            src_ref=src, dst_ref=dst, send_sem=send, recv_sem=recv,
            device_id=device, device_id_type=MESH,
        )
        copy.start()
        return copy

    def send_in(q):
        for copy in row_loads[q][:3]:
            copy.wait()
        fill(q, s_x, lambda rows, cols: gi[rows, cols].astype(F32) * va[rows, cols].astype(F32))
        fill(q, s_f, lambda rows, cols: fl[rows, cols])

        @pl.loop(0, n, unroll=2)
        def _(d):
            for i in range(cq):
                pack[q, d, i] = lane_rows(s_x, q, d * cq + i).astype(BF)
                pack[q, d, cq + i] = lane_rows(s_f, q, d * cq + i).astype(BF)

        if q == 0:
            pl.semaphore_wait(barrier, n - 1 + nz - 1)
        copies = []
        for k in range(1, n):
            d = lax.rem(me + k, n)
            copies.append(
                start(pack.at[q, d], got.at[q, me], in_send.at[q, k], in_recv.at[q, k], (d, mz))
            )
        got[q, me] = pack[q, me]
        return copies

    def send_out(q):
        for copy in in_copies[q]:
            copy.wait_recv()
        for i in range(cq):
            x = got[q, :, i].reshape(n * tiles, LANES)
            f = got[q, :, cq + i].reshape(n * tiles, LANES)
            y = convolve(x, f, fa[...], fb[...], gb[...], ga[...], tc[...], ts[...])
            conv[q, :, i] = y.astype(BF).reshape(n, tiles, LANES)
        copies = []
        for k in range(1, n):
            d = lax.rem(me + k, n)
            copies.append(
                start(conv.at[q, d], cin.at[q, me], out_send.at[q, k], out_recv.at[q, k], (d, mz))
            )
        cin[q, me] = conv[q, me]
        return copies

    def send_z(q):
        row_loads[q][3].wait()
        fill(q, s_g, lambda rows, cols: go[rows, cols].astype(F32))
        for copy in out_copies[q]:
            copy.wait_recv()

        @pl.loop(0, n, unroll=2)
        def _(d):
            for pair in range(cq // 2):
                both = []
                for i in (2 * pair, 2 * pair + 1):
                    c = d * cq + i
                    through = skip[q * group + c] * lane_rows(s_x, q, c)
                    both.append(lane_rows(s_g, q, c) * (cin[q, d, i].astype(F32) + through))
                for z in range(nz):
                    rows = slice(z * quarter, (z + 1) * quarter)
                    gated[q, z, d * (cq // 2) + pair] = jnp.concatenate(
                        [both[0][rows], both[1][rows]], axis=0
                    ).astype(BF)

        copies = []
        for k in range(1, nz):
            z = lax.rem(mz + k, nz)
            copies.append(
                start(gated.at[q, z], rz.at[q, mz], z_send.at[q, k], z_recv.at[q, k], (me, z))
            )
        rz[q, mz] = gated[q, mz]
        return copies

    def finish(q):
        for copy in z_copies[q]:
            copy.wait_recv()
        tall[...] = rz[q].astype(F32).reshape(tall.shape)
        for z in range(nz):
            rows = slice(z * chans + q * group, z * chans + (q + 1) * group)
            for j in range(quarter):
                first = z * group * quarter + j
                out[rows, j * LANES:(j + 1) * LANES] = tall[
                    pl.ds(first, group, stride=quarter), :
                ].astype(BF)

    in_copies, out_copies, z_copies = [], [], []
    for q in range(min(2, parts)):
        in_copies.append(send_in(q))
    for copy in loads[:-1]:
        copy.wait()
    for narrow, wide in ((fa, wide_fa), (fb, wide_fb), (gb, wide_gb), (ga, wide_ga)):
        narrow[...] = wide[...].astype(BF)
    for q in range(parts):
        out_copies.append(send_out(q))
        if q + 2 < parts:
            in_copies.append(send_in(q + 2))
        if q >= 1:
            z_copies.append(send_z(q - 1))
    z_copies.append(send_z(parts - 1))
    for q in range(parts):
        finish(q)
    for copies in in_copies + out_copies + z_copies:
        for copy in copies:
            copy.wait_send()
    loads[-1].wait()


def regroup(n, nz, parts, gate_inner, values, gate_outer, filters, skip_bias, out_weight):
    chans, toks = gate_inner.shape
    tiles = toks // LANES
    cq = chans // n // parts
    quarter = tiles // nz
    operands = (gate_inner, values, filters, gate_outer, skip_bias, *tables(n * tiles))
    fixed = [pltpu.VMEM(a.shape, BF) for a in operands[5:9]]
    dma = pltpu.SemaphoreType.DMA
    local = [pltpu.VMEM(a.shape, a.dtype) for a in operands]
    local[4] = pltpu.SMEM(skip_bias.shape, F32)
    operands += (out_weight,)
    vmem = pl.BlockSpec(memory_space=pltpu.VMEM)
    return pl.pallas_call(
        functools.partial(kernel, n, nz, parts),
        out_shape=(
            jax.ShapeDtypeStruct((nz * chans, toks // nz), BF),
            jax.ShapeDtypeStruct(out_weight.shape, BF),
        ),
        in_specs=[pl.BlockSpec(memory_space=pltpu.HBM)] * len(operands),
        out_specs=(vmem, vmem),
        scratch_shapes=local + fixed + [
            pltpu.VMEM((tiles * chans, LANES), F32),
            pltpu.VMEM((tiles * chans, LANES), F32),
            pltpu.VMEM((tiles * chans, LANES), F32),
            pltpu.VMEM((parts, n, 2 * cq, tiles, LANES), BF),
            pltpu.VMEM((parts, n, 2 * cq, tiles, LANES), BF),
            pltpu.VMEM((parts, n, cq, tiles, LANES), BF),
            pltpu.VMEM((parts, n, cq, tiles, LANES), BF),
            pltpu.VMEM((parts, nz, n * cq // 2, 2 * quarter, LANES), BF),
            pltpu.VMEM((parts, nz, n * cq // 2, 2 * quarter, LANES), BF),
            pltpu.VMEM((nz * n * cq * quarter, LANES), F32),
            dma((parts, 4)),
            dma((8,)),
            dma((parts, n)), dma((parts, n)),
            dma((parts, n)), dma((parts, n)),
            dma((parts, nz)), dma((parts, nz)),
        ],
        compiler_params=pltpu.CompilerParams(
            collective_id=0, has_side_effects=True, vmem_limit_bytes=44 * 2**20
        ),
        name="convolve_and_regroup",
    )(*[pltpu.with_memory_space_constraint(a, pltpu.HBM) for a in operands])


def project_kernel(lhs, weight, out, rows):
    width = out.shape[1]
    j = pl.program_id(0)

    @pl.when(j == 0)
    def _():
        for k in range(rows.shape[0] // LANES):
            part = slice(k * LANES, (k + 1) * LANES)
            rows[part, :] = lhs[:, part].astype(F32).T.astype(BF)

    cols = pl.ds(pl.multiple_of(j * width, width), width)
    out[...] = mm(rows[...], weight[:, cols]).astype(BF)


def project(lhs, weight):
    depth, height = lhs.shape
    width = weight.shape[1]
    block = min(512, width)
    vmem = pl.BlockSpec(memory_space=pltpu.VMEM)
    return pl.pallas_call(
        project_kernel,
        out_shape=jax.ShapeDtypeStruct((height, width), BF),
        grid=(width // block,),
        in_specs=[vmem, vmem],
        out_specs=pl.BlockSpec((height, block), lambda j: (0, j)),
        scratch_shapes=[pltpu.VMEM((height, depth), BF)],
        compiler_params=pltpu.CompilerParams(vmem_limit_bytes=24 * 2**20),
        name="project",
    )(lhs, weight)


def shards(n, nz, gate_inner, values, gate_outer, filters, skip_bias, out_weight):
    parts = max(1, min(4, gate_inner.shape[0] // n // 2))
    lhs, weight = regroup(
        n, nz, parts, gate_inner, values, gate_outer, filters, skip_bias, out_weight
    )
    return project(lhs, weight)


def solution(mesh):
    n, nz = mesh.shape["seq"], mesh.shape["ch"]
    in_specs = (P("ch", "seq"), P("ch", "seq"), P("ch", "seq"), P("ch", "seq"), P("ch"), P())
    out_specs = P(("seq", "ch"), None)
    return jax.shard_map(
        functools.partial(shards, n, nz),
        mesh=mesh, in_specs=in_specs, out_specs=out_specs, check_vma=False,
    )
```

```python
import functools

import jax
import jax.numpy as jnp
import numpy as np
from jax import lax
from jax.experimental import pallas as pl
from jax.experimental.pallas import tpu as pltpu
from jax.sharding import PartitionSpec as P

MESH = pl.DeviceIdType.MESH
LANES = 128
BF = jnp.bfloat16
F32 = jnp.float32


def tables(height):
    length = height * LANES
    low = np.arange(height)
    lane = np.arange(LANES)
    first = 2.0 * np.pi / (4 * height) * ((4 * low[:, None] + 1) * low[None, :] % (4 * height))
    twist = 2.0 * np.pi / (4 * length) * ((4 * low[:, None] + 1) * lane[None, :] % (4 * length))
    second = 2.0 * np.pi / LANES * (lane[:, None] * lane[None, :] % LANES)
    cos2, sin2 = np.cos(second), np.sin(second)
    fa = np.concatenate([np.cos(first), -np.sin(first)], 0)
    fb = np.block([[cos2, -sin2], [sin2, cos2]])
    gb = np.block([[cos2, sin2], [-sin2, cos2]]) / LANES
    ga = np.concatenate([np.cos(first.T), -np.sin(first.T)], 1) / height
    return (
        jnp.asarray(fa, F32),
        jnp.asarray(fb, F32),
        jnp.asarray(gb, F32),
        jnp.asarray(ga, F32),
        jnp.asarray(np.cos(twist), F32),
        jnp.asarray(np.sin(twist), F32),
    )


def mm(a, b):
    return jnp.dot(a, b, preferred_element_type=F32)


def convolve(x, f, fa, fb, gb, ga, tc, ts):
    height = x.shape[0]
    spread = mm(fa, jnp.concatenate([x, f], axis=1))
    xr, fr = spread[:height, :LANES], spread[:height, LANES:]
    xi, fi = spread[height:, :LANES], spread[height:, LANES:]
    rows_x = jnp.concatenate([xr * tc + xi * ts, xi * tc - xr * ts], axis=1)
    rows_f = jnp.concatenate([fr * tc + fi * ts, fi * tc - fr * ts], axis=1)
    sx = mm(rows_x.astype(BF), fb)
    sf = mm(rows_f.astype(BF), fb)
    xr, xi, fr, fi = sx[:, :LANES], sx[:, LANES:], sf[:, :LANES], sf[:, LANES:]
    prod = jnp.concatenate([xr * fr - xi * fi, xr * fi + xi * fr], axis=1).astype(BF)
    back = mm(prod, gb)
    br, bi = back[:, :LANES], back[:, LANES:]
    turned = jnp.concatenate([br * tc - bi * ts, bi * tc + br * ts], axis=0).astype(BF)
    return mm(ga, turned)


def kernel(
    n, nz, parts, *refs,
):
    hbm, (out, weight), rest = refs[:12], refs[12:14], refs[14:]
    gi, va, fl, go, skip, wide_fa, wide_fb, wide_gb, wide_ga, tc, ts = rest[:11]
    fa, fb, gb, ga, s_x, s_f, s_g, pack, got, conv, cin, gated, rz, tall = rest[11:25]
    row_load, load, in_send, in_recv, out_send, out_recv, z_send, z_recv = rest[25:]
    me = lax.axis_index("seq")
    mz = lax.axis_index("ch")
    chans, toks = gi.shape
    tiles = toks // LANES
    own = chans // n
    cq = own // parts
    quarter = tiles // nz
    group = n * cq

    barrier = pltpu.get_barrier_semaphore()
    for k in range(1, n):
        pl.semaphore_signal(barrier, inc=1, device_id=(lax.rem(me + k, n), mz), device_id_type=MESH)
    for k in range(1, nz):
        pl.semaphore_signal(barrier, inc=1, device_id=(me, lax.rem(mz + k, nz)), device_id_type=MESH)
    row_loads = []
    for q in range(parts):
        rows = pl.ds(q * group, group)
        row_loads.append([
            pltpu.make_async_copy(hbm[i].at[rows], rest[i].at[rows], row_load.at[q, i])
            for i in range(4)
        ])
    loads = [pltpu.make_async_copy(hbm[i], rest[i], load.at[i - 4]) for i in range(4, 11)]
    loads.append(pltpu.make_async_copy(hbm[11], weight, load.at[7]))
    for copies in row_loads:
        for copy in copies[:3]:
            copy.start()
    for copy in loads[:-1]:
        copy.start()
    for copies in row_loads:
        copies[3].start()
    loads[-1].start()

    def fill(q, dst, value):
        @pl.loop(0, tiles, unroll=4)
        def _(t):
            cols = pl.ds(pl.multiple_of(t * LANES, LANES), LANES)
            first = pl.multiple_of((q * tiles + t) * group, group)
            dst[pl.ds(first, group), :] = value(pl.ds(q * group, group), cols)

    def lane_rows(src, q, c):
        return src[pl.ds(q * tiles * group + c, tiles, stride=group), :]

    def start(src, dst, send, recv, device):
        copy = pltpu.make_async_remote_copy(
            src_ref=src, dst_ref=dst, send_sem=send, recv_sem=recv,
            device_id=device, device_id_type=MESH,
        )
        copy.start()
        return copy

    def send_in(q):
        for copy in row_loads[q][:3]:
            copy.wait()
        fill(q, s_x, lambda rows, cols: gi[rows, cols].astype(F32) * va[rows, cols].astype(F32))
        fill(q, s_f, lambda rows, cols: fl[rows, cols])

        @pl.loop(0, n, unroll=2)
        def _(d):
            for i in range(cq):
                pack[q, d, i] = lane_rows(s_x, q, d * cq + i).astype(BF)
                pack[q, d, cq + i] = lane_rows(s_f, q, d * cq + i).astype(BF)

        if q == 0:
            pl.semaphore_wait(barrier, n - 1 + nz - 1)
        copies = []
        for k in range(1, n):
            d = lax.rem(me + k, n)
            copies.append(
                start(pack.at[q, d], got.at[q, me], in_send.at[q, k], in_recv.at[q, k], (d, mz))
            )
        got[q, me] = pack[q, me]
        return copies

    def send_out(q):
        for copy in in_copies[q]:
            copy.wait_recv()
        for i in range(cq):
            x = got[q, :, i].reshape(n * tiles, LANES)
            f = got[q, :, cq + i].reshape(n * tiles, LANES)
            y = convolve(x, f, fa[...], fb[...], gb[...], ga[...], tc[...], ts[...])
            conv[q, :, i] = y.astype(BF).reshape(n, tiles, LANES)
        copies = []
        for k in range(1, n):
            d = lax.rem(me + k, n)
            copies.append(
                start(conv.at[q, d], cin.at[q, me], out_send.at[q, k], out_recv.at[q, k], (d, mz))
            )
        cin[q, me] = conv[q, me]
        return copies

    def send_z(q):
        row_loads[q][3].wait()
        fill(q, s_g, lambda rows, cols: go[rows, cols].astype(F32))
        for copy in out_copies[q]:
            copy.wait_recv()

        @pl.loop(0, n, unroll=2)
        def _(d):
            for pair in range(cq // 2):
                both = []
                for i in (2 * pair, 2 * pair + 1):
                    c = d * cq + i
                    through = skip[q * group + c] * lane_rows(s_x, q, c)
                    both.append(lane_rows(s_g, q, c) * (cin[q, d, i].astype(F32) + through))
                for z in range(nz):
                    rows = slice(z * quarter, (z + 1) * quarter)
                    gated[q, z, d * (cq // 2) + pair] = jnp.concatenate(
                        [both[0][rows], both[1][rows]], axis=0
                    ).astype(BF)

        copies = []
        for k in range(1, nz):
            z = lax.rem(mz + k, nz)
            copies.append(
                start(gated.at[q, z], rz.at[q, mz], z_send.at[q, k], z_recv.at[q, k], (me, z))
            )
        rz[q, mz] = gated[q, mz]
        return copies

    def finish(q):
        for copy in z_copies[q]:
            copy.wait_recv()
        tall[...] = rz[q].astype(F32).reshape(tall.shape)
        for z in range(nz):
            rows = slice(z * chans + q * group, z * chans + (q + 1) * group)
            for j in range(quarter):
                first = z * group * quarter + j
                out[rows, j * LANES:(j + 1) * LANES] = tall[
                    pl.ds(first, group, stride=quarter), :
                ].astype(BF)

    in_copies, out_copies, z_copies = [], [], []
    for q in range(min(3, parts)):
        in_copies.append(send_in(q))
    for copy in loads[:-1]:
        copy.wait()
    for narrow, wide in ((fa, wide_fa), (fb, wide_fb), (gb, wide_gb), (ga, wide_ga)):
        narrow[...] = wide[...].astype(BF)
    for q in range(parts):
        out_copies.append(send_out(q))
        if q + 3 < parts:
            in_copies.append(send_in(q + 3))
        if q >= 1:
            z_copies.append(send_z(q - 1))
    z_copies.append(send_z(parts - 1))
    for q in range(parts):
        finish(q)
    for copies in in_copies + out_copies + z_copies:
        for copy in copies:
            copy.wait_send()
    loads[-1].wait()


def regroup(n, nz, parts, gate_inner, values, gate_outer, filters, skip_bias, out_weight):
    chans, toks = gate_inner.shape
    tiles = toks // LANES
    cq = chans // n // parts
    quarter = tiles // nz
    operands = (gate_inner, values, filters, gate_outer, skip_bias, *tables(n * tiles))
    fixed = [pltpu.VMEM(a.shape, BF) for a in operands[5:9]]
    dma = pltpu.SemaphoreType.DMA
    local = [pltpu.VMEM(a.shape, a.dtype) for a in operands]
    local[4] = pltpu.SMEM(skip_bias.shape, F32)
    operands += (out_weight,)
    vmem = pl.BlockSpec(memory_space=pltpu.VMEM)
    return pl.pallas_call(
        functools.partial(kernel, n, nz, parts),
        out_shape=(
            jax.ShapeDtypeStruct((nz * chans, toks // nz), BF),
            jax.ShapeDtypeStruct(out_weight.shape, BF),
        ),
        in_specs=[pl.BlockSpec(memory_space=pltpu.HBM)] * len(operands),
        out_specs=(vmem, vmem),
        scratch_shapes=local + fixed + [
            pltpu.VMEM((tiles * chans, LANES), F32),
            pltpu.VMEM((tiles * chans, LANES), F32),
            pltpu.VMEM((tiles * chans, LANES), F32),
            pltpu.VMEM((parts, n, 2 * cq, tiles, LANES), BF),
            pltpu.VMEM((parts, n, 2 * cq, tiles, LANES), BF),
            pltpu.VMEM((parts, n, cq, tiles, LANES), BF),
            pltpu.VMEM((parts, n, cq, tiles, LANES), BF),
            pltpu.VMEM((parts, nz, n * cq // 2, 2 * quarter, LANES), BF),
            pltpu.VMEM((parts, nz, n * cq // 2, 2 * quarter, LANES), BF),
            pltpu.VMEM((nz * n * cq * quarter, LANES), F32),
            dma((parts, 4)),
            dma((8,)),
            dma((parts, n)), dma((parts, n)),
            dma((parts, n)), dma((parts, n)),
            dma((parts, nz)), dma((parts, nz)),
        ],
        compiler_params=pltpu.CompilerParams(
            collective_id=0, has_side_effects=True, vmem_limit_bytes=44 * 2**20
        ),
        name="convolve_and_regroup",
    )(*[pltpu.with_memory_space_constraint(a, pltpu.HBM) for a in operands])


def project_kernel(lhs, weight, out, rows):
    width = out.shape[1]
    j = pl.program_id(0)

    @pl.when(j == 0)
    def _():
        for k in range(rows.shape[0] // LANES):
            part = slice(k * LANES, (k + 1) * LANES)
            rows[part, :] = lhs[:, part].astype(F32).T.astype(BF)

    cols = pl.ds(pl.multiple_of(j * width, width), width)
    out[...] = mm(rows[...], weight[:, cols]).astype(BF)


def project(lhs, weight):
    depth, height = lhs.shape
    width = weight.shape[1]
    block = min(256, width)
    vmem = pl.BlockSpec(memory_space=pltpu.VMEM)
    return pl.pallas_call(
        project_kernel,
        out_shape=jax.ShapeDtypeStruct((height, width), BF),
        grid=(width // block,),
        in_specs=[vmem, vmem],
        out_specs=pl.BlockSpec((height, block), lambda j: (0, j)),
        scratch_shapes=[pltpu.VMEM((height, depth), BF)],
        compiler_params=pltpu.CompilerParams(vmem_limit_bytes=24 * 2**20),
        name="project",
    )(lhs, weight)


def shards(n, nz, gate_inner, values, gate_outer, filters, skip_bias, out_weight):
    parts = max(1, min(4, gate_inner.shape[0] // n // 2))
    lhs, weight = regroup(
        n, nz, parts, gate_inner, values, gate_outer, filters, skip_bias, out_weight
    )
    return project(lhs, weight)


def solution(mesh):
    n, nz = mesh.shape["seq"], mesh.shape["ch"]
    in_specs = (P("ch", "seq"), P("ch", "seq"), P("ch", "seq"), P("ch", "seq"), P("ch"), P())
    out_specs = P(("seq", "ch"), None)
    return jax.shard_map(
        functools.partial(shards, n, nz),
        mesh=mesh, in_specs=in_specs, out_specs=out_specs, check_vma=False,
    )
```

```python
import functools

import jax
import jax.numpy as jnp
import numpy as np
from jax import lax
from jax.experimental import pallas as pl
from jax.experimental.pallas import tpu as pltpu
from jax.sharding import PartitionSpec as P

MESH = pl.DeviceIdType.MESH
LANES = 128
BF = jnp.bfloat16
F32 = jnp.float32


def tables(height):
    length = height * LANES
    low = np.arange(height)
    lane = np.arange(LANES)
    first = 2.0 * np.pi / (4 * height) * ((4 * low[:, None] + 1) * low[None, :] % (4 * height))
    twist = 2.0 * np.pi / (4 * length) * ((4 * low[:, None] + 1) * lane[None, :] % (4 * length))
    second = 2.0 * np.pi / LANES * (lane[:, None] * lane[None, :] % LANES)
    cos2, sin2 = np.cos(second), np.sin(second)
    fa = np.concatenate([np.cos(first), -np.sin(first)], 0)
    fb = np.block([[cos2, -sin2], [sin2, cos2]])
    gb = np.block([[cos2, sin2], [-sin2, cos2]]) / LANES
    ga = np.concatenate([np.cos(first.T), -np.sin(first.T)], 1) / height
    return (
        jnp.asarray(fa, F32),
        jnp.asarray(fb, F32),
        jnp.asarray(gb, F32),
        jnp.asarray(ga, F32),
        jnp.asarray(np.cos(twist), F32),
        jnp.asarray(np.sin(twist), F32),
    )


def mm(a, b):
    return jnp.dot(a, b, preferred_element_type=F32)


def convolve(x, f, fa, fb, gb, ga, tc, ts):
    height = x.shape[0]
    spread = mm(fa, jnp.concatenate([x, f], axis=1))
    xr, fr = spread[:height, :LANES], spread[:height, LANES:]
    xi, fi = spread[height:, :LANES], spread[height:, LANES:]
    rows_x = jnp.concatenate([xr * tc + xi * ts, xi * tc - xr * ts], axis=1)
    rows_f = jnp.concatenate([fr * tc + fi * ts, fi * tc - fr * ts], axis=1)
    sx = mm(rows_x.astype(BF), fb)
    sf = mm(rows_f.astype(BF), fb)
    xr, xi, fr, fi = sx[:, :LANES], sx[:, LANES:], sf[:, :LANES], sf[:, LANES:]
    prod = jnp.concatenate([xr * fr - xi * fi, xr * fi + xi * fr], axis=1).astype(BF)
    back = mm(prod, gb)
    br, bi = back[:, :LANES], back[:, LANES:]
    turned = jnp.concatenate([br * tc - bi * ts, bi * tc + br * ts], axis=0).astype(BF)
    return mm(ga, turned)


def kernel(
    n, nz, parts, subs, *refs,
):
    hbm, (out, weight), rest = refs[:12], refs[12:14], refs[14:]
    gi, va, fl, go, skip, wide_fa, wide_fb, wide_gb, wide_ga, tc, ts = rest[:11]
    fa, fb, gb, ga, s_x, s_f, s_g, pack, got, conv, cin, gated, rz, tall = rest[11:25]
    row_load, load, in_send, in_recv, out_send, out_recv, z_send, z_recv = rest[25:]
    me = lax.axis_index("seq")
    mz = lax.axis_index("ch")
    chans, toks = gi.shape
    tiles = toks // LANES
    quarter = tiles // nz
    group = n * subs
    chunks = parts * subs

    barrier = pltpu.get_barrier_semaphore()
    for k in range(1, n):
        pl.semaphore_signal(barrier, inc=1, device_id=(lax.rem(me + k, n), mz), device_id_type=MESH)
    for k in range(1, nz):
        pl.semaphore_signal(barrier, inc=1, device_id=(me, lax.rem(mz + k, nz)), device_id_type=MESH)
    row_loads = []
    for q in range(parts):
        rows = pl.ds(q * group, group)
        row_loads.append([
            pltpu.make_async_copy(hbm[i].at[rows], rest[i].at[rows], row_load.at[q, i])
            for i in range(4)
        ])
    loads = [pltpu.make_async_copy(hbm[i], rest[i], load.at[i - 4]) for i in range(4, 11)]
    loads.append(pltpu.make_async_copy(hbm[11], weight, load.at[7]))
    for copies in row_loads:
        for copy in copies[:3]:
            copy.start()
    for copy in loads[:-1]:
        copy.start()
    for copies in row_loads:
        copies[3].start()
    loads[-1].start()

    def fill(q, dst, value):
        @pl.loop(0, tiles, unroll=4)
        def _(t):
            cols = pl.ds(pl.multiple_of(t * LANES, LANES), LANES)
            first = pl.multiple_of((q * tiles + t) * group, group)
            dst[pl.ds(first, group), :] = value(pl.ds(q * group, group), cols)

    def lane_rows(src, q, d):
        first = q // subs * tiles * group + q % subs * n
        return src[pl.ds(first + d, tiles, stride=group), :]

    def start(src, dst, send, recv, device):
        copy = pltpu.make_async_remote_copy(
            src_ref=src, dst_ref=dst, send_sem=send, recv_sem=recv,
            device_id=device, device_id_type=MESH,
        )
        copy.start()
        return copy

    def send_in(q):
        g = q // subs
        if q % subs == 0:
            for copy in row_loads[g][:3]:
                copy.wait()
            fill(g, s_x, lambda rows, cols: gi[rows, cols].astype(F32) * va[rows, cols].astype(F32))
            fill(g, s_f, lambda rows, cols: fl[rows, cols])

        @pl.loop(0, n, unroll=2)
        def _(d):
            pack[q, d, 0] = lane_rows(s_x, q, d).astype(BF)
            pack[q, d, 1] = lane_rows(s_f, q, d).astype(BF)

        if q == 0:
            pl.semaphore_wait(barrier, n - 1 + nz - 1)
        copies = []
        for k in range(1, n):
            d = lax.rem(me + k, n)
            copies.append(
                start(pack.at[q, d], got.at[q, me], in_send.at[q, k], in_recv.at[q, k], (d, mz))
            )
        got[q, me] = pack[q, me]
        return copies

    def send_out(q):
        for copy in in_copies[q]:
            copy.wait_recv()
        x = got[q, :, 0].reshape(n * tiles, LANES)
        f = got[q, :, 1].reshape(n * tiles, LANES)
        y = convolve(x, f, fa[...], fb[...], gb[...], ga[...], tc[...], ts[...])
        conv[q] = y.astype(BF).reshape(n, tiles, LANES)
        copies = []
        for k in range(1, n):
            d = lax.rem(me + k, n)
            copies.append(
                start(conv.at[q, d], cin.at[q, me], out_send.at[q, k], out_recv.at[q, k], (d, mz))
            )
        cin[q, me] = conv[q, me]
        return copies

    def send_z(q):
        g = q // subs
        if q % subs == 0:
            row_loads[g][3].wait()
            fill(g, s_g, lambda rows, cols: go[rows, cols].astype(F32))
        for copy in out_copies[q]:
            copy.wait_recv()

        @pl.loop(0, n // 2, unroll=2)
        def _(pair):
            both = []
            for d in (2 * pair, 2 * pair + 1):
                through = skip[q * n + d] * lane_rows(s_x, q, d)
                both.append(lane_rows(s_g, q, d) * (cin[q, d].astype(F32) + through))
            for z in range(nz):
                rows = slice(z * quarter, (z + 1) * quarter)
                gated[q, z, pair] = jnp.concatenate([both[0][rows], both[1][rows]], axis=0).astype(BF)

        copies = []
        for k in range(1, nz):
            z = lax.rem(mz + k, nz)
            copies.append(
                start(gated.at[q, z], rz.at[q, mz], z_send.at[q, k], z_recv.at[q, k], (me, z))
            )
        rz[q, mz] = gated[q, mz]
        return copies

    def finish(g):
        for i in range(subs):
            q = g * subs + i
            for copy in z_copies[q]:
                copy.wait_recv()
            for z in range(nz):
                rows = slice((z * subs + i) * n * quarter, (z * subs + i + 1) * n * quarter)
                tall[rows, :] = rz[q, z].astype(F32).reshape(n * quarter, LANES)
        for z in range(nz):
            rows = slice(z * chans + g * group, z * chans + (g + 1) * group)
            for j in range(quarter):
                first = z * group * quarter + j
                out[rows, j * LANES:(j + 1) * LANES] = tall[
                    pl.ds(first, group, stride=quarter), :
                ].astype(BF)

    in_copies, out_copies, z_copies = [], [], []
    ahead = min(4, chunks)
    for q in range(ahead):
        in_copies.append(send_in(q))
    for copy in loads[:-1]:
        copy.wait()
    for narrow, wide in ((fa, wide_fa), (fb, wide_fb), (gb, wide_gb), (ga, wide_ga)):
        narrow[...] = wide[...].astype(BF)
    for q in range(chunks):
        out_copies.append(send_out(q))
        if q + ahead < chunks:
            in_copies.append(send_in(q + ahead))
        if q >= 1:
            z_copies.append(send_z(q - 1))
    z_copies.append(send_z(chunks - 1))
    for g in range(parts):
        finish(g)
    for copies in in_copies + out_copies + z_copies:
        for copy in copies:
            copy.wait_send()
    loads[-1].wait()


def regroup(n, nz, parts, subs, gate_inner, values, gate_outer, filters, skip_bias, out_weight):
    chans, toks = gate_inner.shape
    tiles = toks // LANES
    chunks = parts * subs
    quarter = tiles // nz
    operands = (gate_inner, values, filters, gate_outer, skip_bias, *tables(n * tiles))
    fixed = [pltpu.VMEM(a.shape, BF) for a in operands[5:9]]
    dma = pltpu.SemaphoreType.DMA
    local = [pltpu.VMEM(a.shape, a.dtype) for a in operands]
    local[4] = pltpu.SMEM(skip_bias.shape, F32)
    operands += (out_weight,)
    vmem = pl.BlockSpec(memory_space=pltpu.VMEM)
    return pl.pallas_call(
        functools.partial(kernel, n, nz, parts, subs),
        out_shape=(
            jax.ShapeDtypeStruct((nz * chans, toks // nz), BF),
            jax.ShapeDtypeStruct(out_weight.shape, BF),
        ),
        in_specs=[pl.BlockSpec(memory_space=pltpu.HBM)] * len(operands),
        out_specs=(vmem, vmem),
        scratch_shapes=local + fixed + [
            pltpu.VMEM((tiles * chans, LANES), F32),
            pltpu.VMEM((tiles * chans, LANES), F32),
            pltpu.VMEM((tiles * chans, LANES), F32),
            pltpu.VMEM((chunks, n, 2, tiles, LANES), BF),
            pltpu.VMEM((chunks, n, 2, tiles, LANES), BF),
            pltpu.VMEM((chunks, n, tiles, LANES), BF),
            pltpu.VMEM((chunks, n, tiles, LANES), BF),
            pltpu.VMEM((chunks, nz, n // 2, 2 * quarter, LANES), BF),
            pltpu.VMEM((chunks, nz, n // 2, 2 * quarter, LANES), BF),
            pltpu.VMEM((nz * n * subs * quarter, LANES), F32),
            dma((parts, 4)),
            dma((8,)),
            dma((chunks, n)), dma((chunks, n)),
            dma((chunks, n)), dma((chunks, n)),
            dma((chunks, nz)), dma((chunks, nz)),
        ],
        compiler_params=pltpu.CompilerParams(
            collective_id=0, has_side_effects=True, vmem_limit_bytes=44 * 2**20
        ),
        name="convolve_and_regroup",
    )(*[pltpu.with_memory_space_constraint(a, pltpu.HBM) for a in operands])


def project_kernel(lhs, weight, out, rows, done, sem):
    blocks, _, width = done.shape

    @pl.loop(0, rows.shape[0] // LANES, unroll=2)
    def _(k):
        part = pl.ds(pl.multiple_of(k * LANES, LANES), LANES)
        rows[part, :] = lhs[:, part].astype(F32).T.astype(BF)

    def write(j):
        cols = pl.ds(pl.multiple_of(j * width, width), width)
        return pltpu.make_async_copy(done.at[j], out.at[:, cols], sem.at[j])

    @pl.loop(0, blocks)
    def _(j):
        cols = pl.ds(pl.multiple_of(j * width, width), width)
        done[j] = mm(rows[...], weight[:, cols]).astype(BF)
        write(j).start()

    @pl.loop(0, blocks)
    def _(j):
        write(j).wait()


def project(lhs, weight):
    depth, height = lhs.shape
    width = weight.shape[1]
    block = min(512, width)
    vmem = pl.BlockSpec(memory_space=pltpu.VMEM)
    return pl.pallas_call(
        project_kernel,
        out_shape=jax.ShapeDtypeStruct((height, width), BF),
        in_specs=[vmem, vmem],
        out_specs=pl.BlockSpec(memory_space=pltpu.HBM),
        scratch_shapes=[
            pltpu.VMEM((height, depth), BF),
            pltpu.VMEM((width // block, height, block), BF),
            pltpu.SemaphoreType.DMA((width // block,)),
        ],
        compiler_params=pltpu.CompilerParams(vmem_limit_bytes=32 * 2**20),
        name="project",
    )(lhs, weight)


def shards(n, nz, gate_inner, values, gate_outer, filters, skip_bias, out_weight):
    own = gate_inner.shape[0] // n
    parts = max(1, own // 2)
    subs = own // parts
    lhs, weight = regroup(
        n, nz, parts, subs, gate_inner, values, gate_outer, filters, skip_bias, out_weight
    )
    return project(lhs, weight)


def solution(mesh):
    n, nz = mesh.shape["seq"], mesh.shape["ch"]
    in_specs = (P("ch", "seq"), P("ch", "seq"), P("ch", "seq"), P("ch", "seq"), P("ch"), P())
    out_specs = P(("seq", "ch"), None)
    return jax.shard_map(
        functools.partial(shards, n, nz),
        mesh=mesh, in_specs=in_specs, out_specs=out_specs, check_vma=False,
    )
```

```python
import functools

import jax
import jax.numpy as jnp
import numpy as np
from jax import lax
from jax.experimental import pallas as pl
from jax.experimental.pallas import tpu as pltpu
from jax.sharding import PartitionSpec as P

MESH = pl.DeviceIdType.MESH
LANES = 128
BF = jnp.bfloat16
F32 = jnp.float32


def tables(height):
    length = height * LANES
    low = np.arange(height)
    lane = np.arange(LANES)
    first = 2.0 * np.pi / (4 * height) * ((4 * low[:, None] + 1) * low[None, :] % (4 * height))
    twist = 2.0 * np.pi / (4 * length) * ((4 * low[:, None] + 1) * lane[None, :] % (4 * length))
    second = 2.0 * np.pi / LANES * (lane[:, None] * lane[None, :] % LANES)
    cos2, sin2 = np.cos(second), np.sin(second)
    fa = np.concatenate([np.cos(first), -np.sin(first)], 0)
    fb = np.block([[cos2, -sin2], [sin2, cos2]])
    gb = np.block([[cos2, sin2], [-sin2, cos2]]) / LANES
    ga = np.concatenate([np.cos(first.T), -np.sin(first.T)], 1) / height
    return (
        jnp.asarray(fa, F32),
        jnp.asarray(fb, F32),
        jnp.asarray(gb, F32),
        jnp.asarray(ga, F32),
        jnp.asarray(np.cos(twist), F32),
        jnp.asarray(np.sin(twist), F32),
    )


def mm(a, b):
    return jnp.dot(a, b, preferred_element_type=F32)


def convolve(signals, filters, fa, fb, gb, ga, tc, ts):
    height = tc.shape[0]
    count = len(signals)
    spread = mm(fa, jnp.concatenate(signals + filters, axis=1))

    def turn(k):
        re = spread[:height, k * LANES:(k + 1) * LANES]
        im = spread[height:, k * LANES:(k + 1) * LANES]
        return jnp.concatenate([re * tc + im * ts, im * tc - re * ts], axis=1).astype(BF)

    spectra = mm(jnp.concatenate([turn(k) for k in range(2 * count)], axis=0), fb)
    half = count * height
    xr, xi = spectra[:half, :LANES], spectra[:half, LANES:]
    fr, fi = spectra[half:, :LANES], spectra[half:, LANES:]
    prod = jnp.concatenate([xr * fr - xi * fi, xr * fi + xi * fr], axis=1).astype(BF)
    back = mm(prod, gb)
    real, imag = [], []
    for k in range(count):
        br = back[k * height:(k + 1) * height, :LANES]
        bi = back[k * height:(k + 1) * height, LANES:]
        real.append((br * tc - bi * ts).astype(BF))
        imag.append((br * ts + bi * tc).astype(BF))
    turned = jnp.concatenate(
        [jnp.concatenate(real, axis=1), jnp.concatenate(imag, axis=1)], axis=0
    )
    return mm(ga, turned)


def kernel(
    n, nz, parts, *refs,
):
    hbm, (out, weight), rest = refs[:12], refs[12:14], refs[14:]
    gi, va, fl, go, skip, wide_fa, wide_fb, wide_gb, wide_ga, tc, ts = rest[:11]
    fa, fb, gb, ga, s_x, s_f, s_g, pack, got, conv, cin, gated, rz, tall = rest[11:25]
    row_load, load, in_send, in_recv, out_send, out_recv, z_send, z_recv = rest[25:]
    me = lax.axis_index("seq")
    mz = lax.axis_index("ch")
    chans, toks = gi.shape
    tiles = toks // LANES
    own = chans // n
    cq = own // parts
    quarter = tiles // nz
    group = n * cq

    barrier = pltpu.get_barrier_semaphore()
    for k in range(1, n):
        pl.semaphore_signal(barrier, inc=1, device_id=(lax.rem(me + k, n), mz), device_id_type=MESH)
    for k in range(1, nz):
        pl.semaphore_signal(barrier, inc=1, device_id=(me, lax.rem(mz + k, nz)), device_id_type=MESH)
    row_loads = []
    for q in range(parts):
        rows = pl.ds(q * group, group)
        row_loads.append([
            pltpu.make_async_copy(hbm[i].at[rows], rest[i].at[rows], row_load.at[q, i])
            for i in range(4)
        ])
    loads = [pltpu.make_async_copy(hbm[i], rest[i], load.at[i - 4]) for i in range(4, 11)]
    loads.append(pltpu.make_async_copy(hbm[11], weight, load.at[7]))
    for copies in row_loads:
        for copy in copies[:3]:
            copy.start()
    for copy in loads[:-1]:
        copy.start()
    for copies in row_loads:
        copies[3].start()
    loads[-1].start()

    def fill(q, dst, value):
        @pl.loop(0, tiles, unroll=4)
        def _(t):
            cols = pl.ds(pl.multiple_of(t * LANES, LANES), LANES)
            first = pl.multiple_of((q * tiles + t) * group, group)
            dst[pl.ds(first, group), :] = value(pl.ds(q * group, group), cols)

    def lane_rows(src, q, c):
        return src[pl.ds(q * tiles * group + c, tiles, stride=group), :]

    def start(src, dst, send, recv, device):
        copy = pltpu.make_async_remote_copy(
            src_ref=src, dst_ref=dst, send_sem=send, recv_sem=recv,
            device_id=device, device_id_type=MESH,
        )
        copy.start()
        return copy

    def send_in(q):
        for copy in row_loads[q][:3]:
            copy.wait()
        fill(q, s_x, lambda rows, cols: gi[rows, cols].astype(F32) * va[rows, cols].astype(F32))
        fill(q, s_f, lambda rows, cols: fl[rows, cols])

        @pl.loop(0, n, unroll=2)
        def _(d):
            for i in range(cq):
                pack[q, d, i] = lane_rows(s_x, q, d * cq + i).astype(BF)
                pack[q, d, cq + i] = lane_rows(s_f, q, d * cq + i).astype(BF)

        if q == 0:
            pl.semaphore_wait(barrier, n - 1 + nz - 1)
        copies = []
        for k in range(1, n):
            d = lax.rem(me + k, n)
            copies.append(
                start(pack.at[q, d], got.at[q, me], in_send.at[q, k], in_recv.at[q, k], (d, mz))
            )
        got[q, me] = pack[q, me]
        return copies

    def send_out(q):
        for copy in in_copies[q]:
            copy.wait_recv()
        flat = [got[q, :, i].reshape(n * tiles, LANES) for i in range(2 * cq)]
        y = convolve(flat[:cq], flat[cq:], fa[...], fb[...], gb[...], ga[...], tc[...], ts[...])
        for i in range(cq):
            one = y[:, i * LANES:(i + 1) * LANES]
            conv[q, :, i] = one.astype(BF).reshape(n, tiles, LANES)
        copies = []
        for k in range(1, n):
            d = lax.rem(me + k, n)
            copies.append(
                start(conv.at[q, d], cin.at[q, me], out_send.at[q, k], out_recv.at[q, k], (d, mz))
            )
        cin[q, me] = conv[q, me]
        return copies

    def send_z(q):
        row_loads[q][3].wait()
        fill(q, s_g, lambda rows, cols: go[rows, cols].astype(F32))
        for copy in out_copies[q]:
            copy.wait_recv()

        @pl.loop(0, n, unroll=2)
        def _(d):
            for pair in range(cq // 2):
                both = []
                for i in (2 * pair, 2 * pair + 1):
                    c = d * cq + i
                    through = skip[q * group + c] * lane_rows(s_x, q, c)
                    both.append(lane_rows(s_g, q, c) * (cin[q, d, i].astype(F32) + through))
                for z in range(nz):
                    rows = slice(z * quarter, (z + 1) * quarter)
                    gated[q, z, d * (cq // 2) + pair] = jnp.concatenate(
                        [both[0][rows], both[1][rows]], axis=0
                    ).astype(BF)

        copies = []
        for k in range(1, nz):
            z = lax.rem(mz + k, nz)
            copies.append(
                start(gated.at[q, z], rz.at[q, mz], z_send.at[q, k], z_recv.at[q, k], (me, z))
            )
        rz[q, mz] = gated[q, mz]
        return copies

    def finish(q):
        for copy in z_copies[q]:
            copy.wait_recv()
        tall[...] = rz[q].astype(F32).reshape(tall.shape)
        for z in range(nz):
            rows = slice(z * chans + q * group, z * chans + (q + 1) * group)
            for j in range(quarter):
                first = z * group * quarter + j
                out[rows, j * LANES:(j + 1) * LANES] = tall[
                    pl.ds(first, group, stride=quarter), :
                ].astype(BF)

    in_copies, out_copies, z_copies = [], [], []
    for q in range(min(3, parts)):
        in_copies.append(send_in(q))
    for copy in loads[:-1]:
        copy.wait()
    for narrow, wide in ((fa, wide_fa), (fb, wide_fb), (gb, wide_gb), (ga, wide_ga)):
        narrow[...] = wide[...].astype(BF)
    for q in range(parts):
        out_copies.append(send_out(q))
        if q + 3 < parts:
            in_copies.append(send_in(q + 3))
        if q >= 1:
            z_copies.append(send_z(q - 1))
    z_copies.append(send_z(parts - 1))
    for q in range(parts):
        finish(q)
    for copies in in_copies + out_copies + z_copies:
        for copy in copies:
            copy.wait_send()
    loads[-1].wait()


def regroup(n, nz, parts, gate_inner, values, gate_outer, filters, skip_bias, out_weight):
    chans, toks = gate_inner.shape
    tiles = toks // LANES
    cq = chans // n // parts
    quarter = tiles // nz
    operands = (gate_inner, values, filters, gate_outer, skip_bias, *tables(n * tiles))
    fixed = [pltpu.VMEM(a.shape, BF) for a in operands[5:9]]
    dma = pltpu.SemaphoreType.DMA
    local = [pltpu.VMEM(a.shape, a.dtype) for a in operands]
    local[4] = pltpu.SMEM(skip_bias.shape, F32)
    operands += (out_weight,)
    vmem = pl.BlockSpec(memory_space=pltpu.VMEM)
    return pl.pallas_call(
        functools.partial(kernel, n, nz, parts),
        out_shape=(
            jax.ShapeDtypeStruct((nz * chans, toks // nz), BF),
            jax.ShapeDtypeStruct(out_weight.shape, BF),
        ),
        in_specs=[pl.BlockSpec(memory_space=pltpu.HBM)] * len(operands),
        out_specs=(vmem, vmem),
        scratch_shapes=local + fixed + [
            pltpu.VMEM((tiles * chans, LANES), F32),
            pltpu.VMEM((tiles * chans, LANES), F32),
            pltpu.VMEM((tiles * chans, LANES), F32),
            pltpu.VMEM((parts, n, 2 * cq, tiles, LANES), BF),
            pltpu.VMEM((parts, n, 2 * cq, tiles, LANES), BF),
            pltpu.VMEM((parts, n, cq, tiles, LANES), BF),
            pltpu.VMEM((parts, n, cq, tiles, LANES), BF),
            pltpu.VMEM((parts, nz, n * cq // 2, 2 * quarter, LANES), BF),
            pltpu.VMEM((parts, nz, n * cq // 2, 2 * quarter, LANES), BF),
            pltpu.VMEM((nz * n * cq * quarter, LANES), F32),
            dma((parts, 4)),
            dma((8,)),
            dma((parts, n)), dma((parts, n)),
            dma((parts, n)), dma((parts, n)),
            dma((parts, nz)), dma((parts, nz)),
        ],
        compiler_params=pltpu.CompilerParams(
            collective_id=0, has_side_effects=True, vmem_limit_bytes=44 * 2**20
        ),
        name="convolve_and_regroup",
    )(*[pltpu.with_memory_space_constraint(a, pltpu.HBM) for a in operands])


def project_kernel(lhs, weight, out, rows, done, sem):
    blocks, _, width = done.shape

    @pl.loop(0, rows.shape[0] // LANES, unroll=2)
    def _(k):
        part = pl.ds(pl.multiple_of(k * LANES, LANES), LANES)
        rows[part, :] = lhs[:, part].astype(F32).T.astype(BF)

    def write(j):
        cols = pl.ds(pl.multiple_of(j * width, width), width)
        return pltpu.make_async_copy(done.at[j], out.at[:, cols], sem.at[j])

    @pl.loop(0, blocks)
    def _(j):
        cols = pl.ds(pl.multiple_of(j * width, width), width)
        done[j] = mm(rows[...], weight[:, cols]).astype(BF)
        write(j).start()

    @pl.loop(0, blocks)
    def _(j):
        write(j).wait()


def project(lhs, weight):
    depth, height = lhs.shape
    width = weight.shape[1]
    block = min(512, width)
    vmem = pl.BlockSpec(memory_space=pltpu.VMEM)
    return pl.pallas_call(
        project_kernel,
        out_shape=jax.ShapeDtypeStruct((height, width), BF),
        in_specs=[vmem, vmem],
        out_specs=pl.BlockSpec(memory_space=pltpu.HBM),
        scratch_shapes=[
            pltpu.VMEM((height, depth), BF),
            pltpu.VMEM((width // block, height, block), BF),
            pltpu.SemaphoreType.DMA((width // block,)),
        ],
        compiler_params=pltpu.CompilerParams(vmem_limit_bytes=32 * 2**20),
        name="project",
    )(lhs, weight)


def shards(n, nz, gate_inner, values, gate_outer, filters, skip_bias, out_weight):
    parts = max(1, min(4, gate_inner.shape[0] // n // 2))
    lhs, weight = regroup(
        n, nz, parts, gate_inner, values, gate_outer, filters, skip_bias, out_weight
    )
    return project(lhs, weight)


def solution(mesh):
    n, nz = mesh.shape["seq"], mesh.shape["ch"]
    in_specs = (P("ch", "seq"), P("ch", "seq"), P("ch", "seq"), P("ch", "seq"), P("ch"), P())
    out_specs = P(("seq", "ch"), None)
    return jax.shard_map(
        functools.partial(shards, n, nz),
        mesh=mesh, in_specs=in_specs, out_specs=out_specs, check_vma=False,
    )
```

```python
import functools

import jax
import jax.numpy as jnp
import numpy as np
from jax import lax
from jax.experimental import pallas as pl
from jax.experimental.pallas import tpu as pltpu
from jax.sharding import PartitionSpec as P

MESH = pl.DeviceIdType.MESH
LANES = 128
BF = jnp.bfloat16
F32 = jnp.float32


def tables(height):
    length = height * LANES
    low = np.arange(height)
    lane = np.arange(LANES)
    first = 2.0 * np.pi / (4 * height) * ((4 * low[:, None] + 1) * low[None, :] % (4 * height))
    twist = 2.0 * np.pi / (4 * length) * ((4 * low[:, None] + 1) * lane[None, :] % (4 * length))
    second = 2.0 * np.pi / LANES * (lane[:, None] * lane[None, :] % LANES)
    cos2, sin2 = np.cos(second), np.sin(second)
    fa = np.concatenate([np.cos(first), -np.sin(first)], 0)
    fb = np.block([[cos2, -sin2], [sin2, cos2]])
    gb = np.block([[cos2, sin2], [-sin2, cos2]]) / LANES
    ga = np.concatenate([np.cos(first.T), -np.sin(first.T)], 1) / height
    return (
        jnp.asarray(fa, F32),
        jnp.asarray(fb, F32),
        jnp.asarray(gb, F32),
        jnp.asarray(ga, F32),
        jnp.asarray(np.cos(twist), F32),
        jnp.asarray(np.sin(twist), F32),
    )


def mm(a, b):
    return jnp.dot(a, b, preferred_element_type=F32)


def convolve(signals, filters, fa, fb, gb, ga, tc, ts):
    height = tc.shape[0]
    count = len(signals)
    spread = mm(fa, jnp.concatenate(signals + filters, axis=1))

    def turn(k):
        re = spread[:height, k * LANES:(k + 1) * LANES]
        im = spread[height:, k * LANES:(k + 1) * LANES]
        return jnp.concatenate([re * tc + im * ts, im * tc - re * ts], axis=1).astype(BF)

    spectra = mm(jnp.concatenate([turn(k) for k in range(2 * count)], axis=0), fb)
    half = count * height
    xr, xi = spectra[:half, :LANES], spectra[:half, LANES:]
    fr, fi = spectra[half:, :LANES], spectra[half:, LANES:]
    prod = jnp.concatenate([xr * fr - xi * fi, xr * fi + xi * fr], axis=1).astype(BF)
    back = mm(prod, gb)
    real, imag = [], []
    for k in range(count):
        br = back[k * height:(k + 1) * height, :LANES]
        bi = back[k * height:(k + 1) * height, LANES:]
        real.append((br * tc - bi * ts).astype(BF))
        imag.append((br * ts + bi * tc).astype(BF))
    turned = jnp.concatenate(
        [jnp.concatenate(real, axis=1), jnp.concatenate(imag, axis=1)], axis=0
    )
    return mm(ga, turned)


def kernel(
    n, nz, parts, *refs,
):
    hbm, (out, weight), rest = refs[:12], refs[12:14], refs[14:]
    gi, va, fl, go, skip, wide_fa, wide_fb, wide_gb, wide_ga, tc, ts = rest[:11]
    fa, fb, gb, ga, s_x, s_f, s_g, pack, got, conv, cin, gated, rz, tall = rest[11:25]
    row_load, load, in_send, in_recv, out_send, out_recv, z_send, z_recv = rest[25:]
    me = lax.axis_index("seq")
    mz = lax.axis_index("ch")
    chans, toks = gi.shape
    tiles = toks // LANES
    own = chans // n
    cq = own // parts
    quarter = tiles // nz
    group = n * cq

    barrier = pltpu.get_barrier_semaphore()
    for k in range(1, n):
        pl.semaphore_signal(barrier, inc=1, device_id=(lax.rem(me + k, n), mz), device_id_type=MESH)
    for k in range(1, nz):
        pl.semaphore_signal(barrier, inc=1, device_id=(me, lax.rem(mz + k, nz)), device_id_type=MESH)
    row_loads = []
    for q in range(parts):
        rows = pl.ds(q * group, group)
        row_loads.append([
            pltpu.make_async_copy(hbm[i].at[rows], rest[i].at[rows], row_load.at[q, i])
            for i in range(4)
        ])
    loads = [pltpu.make_async_copy(hbm[i], rest[i], load.at[i - 4]) for i in range(4, 11)]
    loads.append(pltpu.make_async_copy(hbm[11], weight, load.at[7]))
    for copies in row_loads:
        for copy in copies[:3]:
            copy.start()
    for copy in loads[:-1]:
        copy.start()
    for copies in row_loads:
        copies[3].start()
    loads[-1].start()

    def fill(q, dst, value):
        @pl.loop(0, tiles, unroll=4)
        def _(t):
            cols = pl.ds(pl.multiple_of(t * LANES, LANES), LANES)
            first = pl.multiple_of((q * tiles + t) * group, group)
            dst[pl.ds(first, group), :] = value(pl.ds(q * group, group), cols)

    def lane_rows(src, q, c):
        return src[pl.ds(q * tiles * group + c, tiles, stride=group), :]

    def start(src, dst, send, recv, device):
        copy = pltpu.make_async_remote_copy(
            src_ref=src, dst_ref=dst, send_sem=send, recv_sem=recv,
            device_id=device, device_id_type=MESH,
        )
        copy.start()
        return copy

    def send_in(q):
        for copy in row_loads[q][:3]:
            copy.wait()
        fill(q, s_x, lambda rows, cols: gi[rows, cols].astype(F32) * va[rows, cols].astype(F32))
        fill(q, s_f, lambda rows, cols: fl[rows, cols])

        @pl.loop(0, n, unroll=2)
        def _(d):
            for i in range(cq):
                pack[q, d, i] = lane_rows(s_x, q, d * cq + i).astype(BF)
                pack[q, d, cq + i] = lane_rows(s_f, q, d * cq + i).astype(BF)

        if q == 0:
            pl.semaphore_wait(barrier, n - 1 + nz - 1)
        copies = []
        for k in range(1, n):
            d = lax.rem(me + k, n)
            copies.append(
                start(pack.at[q, d], got.at[q, me], in_send.at[q, k], in_recv.at[q, k], (d, mz))
            )
        got[q, me] = pack[q, me]
        return copies

    def send_out(q):
        for copy in in_copies[q]:
            copy.wait_recv()
        flat = [got[q, :, i].reshape(n * tiles, LANES) for i in range(2 * cq)]
        y = convolve(flat[:cq], flat[cq:], fa[...], fb[...], gb[...], ga[...], tc[...], ts[...])
        for i in range(cq):
            one = y[:, i * LANES:(i + 1) * LANES]
            conv[q, :, i] = one.astype(BF).reshape(n, tiles, LANES)
        copies = []
        for k in range(1, n):
            d = lax.rem(me + k, n)
            copies.append(
                start(conv.at[q, d], cin.at[q, me], out_send.at[q, k], out_recv.at[q, k], (d, mz))
            )
        cin[q, me] = conv[q, me]
        return copies

    def send_z(q):
        row_loads[q][3].wait()
        fill(q, s_g, lambda rows, cols: go[rows, cols].astype(F32))
        for copy in out_copies[q]:
            copy.wait_recv()

        @pl.loop(0, n, unroll=2)
        def _(d):
            for pair in range(cq // 2):
                both = []
                for i in (2 * pair, 2 * pair + 1):
                    c = d * cq + i
                    through = skip[q * group + c] * lane_rows(s_x, q, c)
                    both.append(lane_rows(s_g, q, c) * (cin[q, d, i].astype(F32) + through))
                for z in range(nz):
                    rows = slice(z * quarter, (z + 1) * quarter)
                    gated[q, z, d * (cq // 2) + pair] = jnp.concatenate(
                        [both[0][rows], both[1][rows]], axis=0
                    ).astype(BF)

        copies = []
        for k in range(1, nz):
            z = lax.rem(mz + k, nz)
            copies.append(
                start(gated.at[q, z], rz.at[q, mz], z_send.at[q, k], z_recv.at[q, k], (me, z))
            )
        rz[q, mz] = gated[q, mz]
        return copies

    def finish(q):
        for copy in z_copies[q]:
            copy.wait_recv()
        tall[...] = rz[q].astype(F32).reshape(tall.shape)
        for z in range(nz):
            rows = slice(z * chans + q * group, z * chans + (q + 1) * group)
            for j in range(quarter):
                first = z * group * quarter + j
                out[rows, j * LANES:(j + 1) * LANES] = tall[
                    pl.ds(first, group, stride=quarter), :
                ].astype(BF)

    in_copies, out_copies, z_copies = [], [], []
    for q in range(min(3, parts)):
        in_copies.append(send_in(q))
    for copy in loads[:-1]:
        copy.wait()
    for narrow, wide in ((fa, wide_fa), (fb, wide_fb), (gb, wide_gb), (ga, wide_ga)):
        narrow[...] = wide[...].astype(BF)
    for q in range(parts):
        out_copies.append(send_out(q))
        if q + 3 < parts:
            in_copies.append(send_in(q + 3))
        if q >= 2:
            z_copies.append(send_z(q - 2))
    for q in range(max(0, parts - 2), parts):
        z_copies.append(send_z(q))
    for q in range(parts):
        finish(q)
    for copies in in_copies + out_copies + z_copies:
        for copy in copies:
            copy.wait_send()
    loads[-1].wait()


def regroup(n, nz, parts, gate_inner, values, gate_outer, filters, skip_bias, out_weight):
    chans, toks = gate_inner.shape
    tiles = toks // LANES
    cq = chans // n // parts
    quarter = tiles // nz
    operands = (gate_inner, values, filters, gate_outer, skip_bias, *tables(n * tiles))
    fixed = [pltpu.VMEM(a.shape, BF) for a in operands[5:9]]
    dma = pltpu.SemaphoreType.DMA
    local = [pltpu.VMEM(a.shape, a.dtype) for a in operands]
    local[4] = pltpu.SMEM(skip_bias.shape, F32)
    operands += (out_weight,)
    vmem = pl.BlockSpec(memory_space=pltpu.VMEM)
    return pl.pallas_call(
        functools.partial(kernel, n, nz, parts),
        out_shape=(
            jax.ShapeDtypeStruct((nz * chans, toks // nz), BF),
            jax.ShapeDtypeStruct(out_weight.shape, BF),
        ),
        in_specs=[pl.BlockSpec(memory_space=pltpu.HBM)] * len(operands),
        out_specs=(vmem, vmem),
        scratch_shapes=local + fixed + [
            pltpu.VMEM((tiles * chans, LANES), F32),
            pltpu.VMEM((tiles * chans, LANES), F32),
            pltpu.VMEM((tiles * chans, LANES), F32),
            pltpu.VMEM((parts, n, 2 * cq, tiles, LANES), BF),
            pltpu.VMEM((parts, n, 2 * cq, tiles, LANES), BF),
            pltpu.VMEM((parts, n, cq, tiles, LANES), BF),
            pltpu.VMEM((parts, n, cq, tiles, LANES), BF),
            pltpu.VMEM((parts, nz, n * cq // 2, 2 * quarter, LANES), BF),
            pltpu.VMEM((parts, nz, n * cq // 2, 2 * quarter, LANES), BF),
            pltpu.VMEM((nz * n * cq * quarter, LANES), F32),
            dma((parts, 4)),
            dma((8,)),
            dma((parts, n)), dma((parts, n)),
            dma((parts, n)), dma((parts, n)),
            dma((parts, nz)), dma((parts, nz)),
        ],
        compiler_params=pltpu.CompilerParams(
            collective_id=0, has_side_effects=True, vmem_limit_bytes=44 * 2**20
        ),
        name="convolve_and_regroup",
    )(*[pltpu.with_memory_space_constraint(a, pltpu.HBM) for a in operands])


def project_kernel(lhs, weight, out, rows, done, sem):
    blocks, _, width = done.shape

    @pl.loop(0, rows.shape[0] // LANES, unroll=2)
    def _(k):
        part = pl.ds(pl.multiple_of(k * LANES, LANES), LANES)
        rows[part, :] = lhs[:, part].astype(F32).T.astype(BF)

    def write(j):
        cols = pl.ds(pl.multiple_of(j * width, width), width)
        return pltpu.make_async_copy(done.at[j], out.at[:, cols], sem.at[j])

    @pl.loop(0, blocks)
    def _(j):
        cols = pl.ds(pl.multiple_of(j * width, width), width)
        done[j] = mm(rows[...], weight[:, cols]).astype(BF)
        write(j).start()

    @pl.loop(0, blocks)
    def _(j):
        write(j).wait()


def project(lhs, weight):
    depth, height = lhs.shape
    width = weight.shape[1]
    block = min(512, width)
    vmem = pl.BlockSpec(memory_space=pltpu.VMEM)
    return pl.pallas_call(
        project_kernel,
        out_shape=jax.ShapeDtypeStruct((height, width), BF),
        in_specs=[vmem, vmem],
        out_specs=pl.BlockSpec(memory_space=pltpu.HBM),
        scratch_shapes=[
            pltpu.VMEM((height, depth), BF),
            pltpu.VMEM((width // block, height, block), BF),
            pltpu.SemaphoreType.DMA((width // block,)),
        ],
        compiler_params=pltpu.CompilerParams(vmem_limit_bytes=32 * 2**20),
        name="project",
    )(lhs, weight)


def shards(n, nz, gate_inner, values, gate_outer, filters, skip_bias, out_weight):
    parts = max(1, min(4, gate_inner.shape[0] // n // 2))
    lhs, weight = regroup(
        n, nz, parts, gate_inner, values, gate_outer, filters, skip_bias, out_weight
    )
    return project(lhs, weight)


def solution(mesh):
    n, nz = mesh.shape["seq"], mesh.shape["ch"]
    in_specs = (P("ch", "seq"), P("ch", "seq"), P("ch", "seq"), P("ch", "seq"), P("ch"), P())
    out_specs = P(("seq", "ch"), None)
    return jax.shard_map(
        functools.partial(shards, n, nz),
        mesh=mesh, in_specs=in_specs, out_specs=out_specs, check_vma=False,
    )
```

```python
import functools

import jax
import jax.numpy as jnp
import numpy as np
from jax import lax
from jax.experimental import pallas as pl
from jax.experimental.pallas import tpu as pltpu
from jax.sharding import PartitionSpec as P

MESH = pl.DeviceIdType.MESH
LANES = 128
BF = jnp.bfloat16
F32 = jnp.float32


def tables(height):
    length = height * LANES
    low = np.arange(height)
    lane = np.arange(LANES)
    first = 2.0 * np.pi / (4 * height) * ((4 * low[:, None] + 1) * low[None, :] % (4 * height))
    twist = 2.0 * np.pi / (4 * length) * ((4 * low[:, None] + 1) * lane[None, :] % (4 * length))
    second = 2.0 * np.pi / LANES * (lane[:, None] * lane[None, :] % LANES)
    cos2, sin2 = np.cos(second), np.sin(second)
    fa = np.concatenate([np.cos(first), -np.sin(first)], 0)
    fb = np.block([[cos2, -sin2], [sin2, cos2]])
    gb = np.block([[cos2, sin2], [-sin2, cos2]]) / LANES
    ga = np.concatenate([np.cos(first.T), -np.sin(first.T)], 1) / height
    return (
        jnp.asarray(fa, F32),
        jnp.asarray(fb, F32),
        jnp.asarray(gb, F32),
        jnp.asarray(ga, F32),
        jnp.asarray(np.cos(twist), F32),
        jnp.asarray(np.sin(twist), F32),
    )


def mm(a, b):
    return jnp.dot(a, b, preferred_element_type=F32)


def convolve(signals, filters, fa, fb, gb, ga, tc, ts):
    height = tc.shape[0]
    count = len(signals)
    spread = mm(fa, jnp.concatenate(signals + filters, axis=1))

    def turn(k):
        re = spread[:height, k * LANES:(k + 1) * LANES]
        im = spread[height:, k * LANES:(k + 1) * LANES]
        return jnp.concatenate([re * tc + im * ts, im * tc - re * ts], axis=1).astype(BF)

    spectra = mm(jnp.concatenate([turn(k) for k in range(2 * count)], axis=0), fb)
    half = count * height
    xr, xi = spectra[:half, :LANES], spectra[:half, LANES:]
    fr, fi = spectra[half:, :LANES], spectra[half:, LANES:]
    prod = jnp.concatenate([xr * fr - xi * fi, xr * fi + xi * fr], axis=1).astype(BF)
    back = mm(prod, gb)
    real, imag = [], []
    for k in range(count):
        br = back[k * height:(k + 1) * height, :LANES]
        bi = back[k * height:(k + 1) * height, LANES:]
        real.append((br * tc - bi * ts).astype(BF))
        imag.append((br * ts + bi * tc).astype(BF))
    turned = jnp.concatenate(
        [jnp.concatenate(real, axis=1), jnp.concatenate(imag, axis=1)], axis=0
    )
    return mm(ga, turned)


def kernel(
    n, nz, parts, *refs,
):
    hbm, (out, weight), rest = refs[:12], refs[12:14], refs[14:]
    gi, va, fl, go, skip, wide_fa, wide_fb, wide_gb, wide_ga, tc, ts = rest[:11]
    fa, fb, gb, ga, s_x, s_f, s_g, pack, got, conv, cin, gated, rz, tall = rest[11:25]
    row_load, load, in_send, in_recv, out_send, out_recv, z_send, z_recv = rest[25:]
    me = lax.axis_index("seq")
    mz = lax.axis_index("ch")
    chans, toks = gi.shape
    tiles = toks // LANES
    own = chans // n
    cq = own // parts
    quarter = tiles // nz
    group = n * cq

    barrier = pltpu.get_barrier_semaphore()
    for k in range(1, n):
        pl.semaphore_signal(barrier, inc=1, device_id=(lax.rem(me + k, n), mz), device_id_type=MESH)
    for k in range(1, nz):
        pl.semaphore_signal(barrier, inc=1, device_id=(me, lax.rem(mz + k, nz)), device_id_type=MESH)
    row_loads = []
    for q in range(parts):
        rows = pl.ds(q * group, group)
        row_loads.append([
            pltpu.make_async_copy(hbm[i].at[rows], rest[i].at[rows], row_load.at[q, i])
            for i in range(4)
        ])
    loads = [pltpu.make_async_copy(hbm[i], rest[i], load.at[i - 4]) for i in range(4, 11)]
    loads.append(pltpu.make_async_copy(hbm[11], weight, load.at[7]))
    for copies in row_loads:
        for copy in copies[:3]:
            copy.start()
    for copy in loads[:-1]:
        copy.start()
    for copies in row_loads:
        copies[3].start()
    loads[-1].start()

    def fill(q, dst, value):
        @pl.loop(0, tiles, unroll=4)
        def _(t):
            cols = pl.ds(pl.multiple_of(t * LANES, LANES), LANES)
            first = pl.multiple_of((q * tiles + t) * group, group)
            dst[pl.ds(first, group), :] = value(pl.ds(q * group, group), cols)

    def lane_rows(src, q, c):
        return src[pl.ds(q * tiles * group + c, tiles, stride=group), :]

    def start(src, dst, send, recv, device):
        copy = pltpu.make_async_remote_copy(
            src_ref=src, dst_ref=dst, send_sem=send, recv_sem=recv,
            device_id=device, device_id_type=MESH,
        )
        copy.start()
        return copy

    def send_in(q):
        for copy in row_loads[q][:3]:
            copy.wait()
        fill(q, s_x, lambda rows, cols: gi[rows, cols].astype(F32) * va[rows, cols].astype(F32))
        fill(q, s_f, lambda rows, cols: fl[rows, cols])

        @pl.loop(0, n, unroll=2)
        def _(d):
            for i in range(cq):
                pack[q, d, i] = lane_rows(s_x, q, d * cq + i).astype(BF)
                pack[q, d, cq + i] = lane_rows(s_f, q, d * cq + i).astype(BF)

        if q == 0:
            pl.semaphore_wait(barrier, n - 1 + nz - 1)
        copies = []
        for k in range(1, n):
            d = lax.rem(me + k, n)
            copies.append(
                start(pack.at[q, d], got.at[q, me], in_send.at[q, k], in_recv.at[q, k], (d, mz))
            )
        got[q, me] = pack[q, me]
        return copies

    def send_out(q):
        for copy in in_copies[q]:
            copy.wait_recv()
        flat = [got[q, :, i].reshape(n * tiles, LANES) for i in range(2 * cq)]
        y = convolve(flat[:cq], flat[cq:], fa[...], fb[...], gb[...], ga[...], tc[...], ts[...])
        for i in range(cq):
            one = y[:, i * LANES:(i + 1) * LANES]
            conv[q, :, i] = one.astype(BF).reshape(n, tiles, LANES)
        copies = []
        for k in range(1, n):
            d = lax.rem(me + k, n)
            copies.append(
                start(conv.at[q, d], cin.at[q, me], out_send.at[q, k], out_recv.at[q, k], (d, mz))
            )
        cin[q, me] = conv[q, me]
        return copies

    def send_z(q):
        row_loads[q][3].wait()
        fill(q, s_g, lambda rows, cols: go[rows, cols].astype(F32))
        for copy in out_copies[q]:
            copy.wait_recv()

        @pl.loop(0, n, unroll=2)
        def _(d):
            for pair in range(cq // 2):
                both = []
                for i in (2 * pair, 2 * pair + 1):
                    c = d * cq + i
                    through = skip[q * group + c] * lane_rows(s_x, q, c)
                    both.append(lane_rows(s_g, q, c) * (cin[q, d, i].astype(F32) + through))
                for z in range(nz):
                    rows = slice(z * quarter, (z + 1) * quarter)
                    gated[q, z, d * (cq // 2) + pair] = jnp.concatenate(
                        [both[0][rows], both[1][rows]], axis=0
                    ).astype(BF)

        copies = []
        for k in range(1, nz):
            z = lax.rem(mz + k, nz)
            copies.append(
                start(gated.at[q, z], rz.at[q, mz], z_send.at[q, k], z_recv.at[q, k], (me, z))
            )
        rz[q, mz] = gated[q, mz]
        return copies

    def finish(q):
        for copy in z_copies[q]:
            copy.wait_recv()
        tall[...] = rz[q].astype(F32).reshape(tall.shape)
        for z in range(nz):
            rows = slice(z * chans + q * group, z * chans + (q + 1) * group)
            for j in range(quarter):
                first = z * group * quarter + j
                out[rows, j * LANES:(j + 1) * LANES] = tall[
                    pl.ds(first, group, stride=quarter), :
                ].astype(BF)

    in_copies, out_copies, z_copies = [], [], []
    for q in range(min(3, parts)):
        in_copies.append(send_in(q))
    for copy in loads[:-1]:
        copy.wait()
    for narrow, wide in ((fa, wide_fa), (fb, wide_fb), (gb, wide_gb), (ga, wide_ga)):
        narrow[...] = wide[...].astype(BF)
    for q in range(parts):
        out_copies.append(send_out(q))
        if q >= 1 and q + 2 < parts:
            in_copies.append(send_in(q + 2))
        if q >= 1:
            z_copies.append(send_z(q - 1))
    z_copies.append(send_z(parts - 1))
    for q in range(parts):
        finish(q)
    for copies in in_copies + out_copies + z_copies:
        for copy in copies:
            copy.wait_send()
    loads[-1].wait()


def regroup(n, nz, parts, gate_inner, values, gate_outer, filters, skip_bias, out_weight):
    chans, toks = gate_inner.shape
    tiles = toks // LANES
    cq = chans // n // parts
    quarter = tiles // nz
    operands = (gate_inner, values, filters, gate_outer, skip_bias, *tables(n * tiles))
    fixed = [pltpu.VMEM(a.shape, BF) for a in operands[5:9]]
    dma = pltpu.SemaphoreType.DMA
    local = [pltpu.VMEM(a.shape, a.dtype) for a in operands]
    local[4] = pltpu.SMEM(skip_bias.shape, F32)
    operands += (out_weight,)
    vmem = pl.BlockSpec(memory_space=pltpu.VMEM)
    return pl.pallas_call(
        functools.partial(kernel, n, nz, parts),
        out_shape=(
            jax.ShapeDtypeStruct((nz * chans, toks // nz), BF),
            jax.ShapeDtypeStruct(out_weight.shape, BF),
        ),
        in_specs=[pl.BlockSpec(memory_space=pltpu.HBM)] * len(operands),
        out_specs=(vmem, vmem),
        scratch_shapes=local + fixed + [
            pltpu.VMEM((tiles * chans, LANES), F32),
            pltpu.VMEM((tiles * chans, LANES), F32),
            pltpu.VMEM((tiles * chans, LANES), F32),
            pltpu.VMEM((parts, n, 2 * cq, tiles, LANES), BF),
            pltpu.VMEM((parts, n, 2 * cq, tiles, LANES), BF),
            pltpu.VMEM((parts, n, cq, tiles, LANES), BF),
            pltpu.VMEM((parts, n, cq, tiles, LANES), BF),
            pltpu.VMEM((parts, nz, n * cq // 2, 2 * quarter, LANES), BF),
            pltpu.VMEM((parts, nz, n * cq // 2, 2 * quarter, LANES), BF),
            pltpu.VMEM((nz * n * cq * quarter, LANES), F32),
            dma((parts, 4)),
            dma((8,)),
            dma((parts, n)), dma((parts, n)),
            dma((parts, n)), dma((parts, n)),
            dma((parts, nz)), dma((parts, nz)),
        ],
        compiler_params=pltpu.CompilerParams(
            collective_id=0, has_side_effects=True, vmem_limit_bytes=44 * 2**20
        ),
        name="convolve_and_regroup",
    )(*[pltpu.with_memory_space_constraint(a, pltpu.HBM) for a in operands])


def project_kernel(lhs, weight, out, rows, done, sem):
    blocks, _, width = done.shape

    @pl.loop(0, rows.shape[0] // LANES, unroll=2)
    def _(k):
        part = pl.ds(pl.multiple_of(k * LANES, LANES), LANES)
        rows[part, :] = lhs[:, part].astype(F32).T.astype(BF)

    def write(j):
        cols = pl.ds(pl.multiple_of(j * width, width), width)
        return pltpu.make_async_copy(done.at[j], out.at[:, cols], sem.at[j])

    @pl.loop(0, blocks)
    def _(j):
        cols = pl.ds(pl.multiple_of(j * width, width), width)
        done[j] = mm(rows[...], weight[:, cols]).astype(BF)
        write(j).start()

    @pl.loop(0, blocks)
    def _(j):
        write(j).wait()


def project(lhs, weight):
    depth, height = lhs.shape
    width = weight.shape[1]
    block = min(512, width)
    vmem = pl.BlockSpec(memory_space=pltpu.VMEM)
    return pl.pallas_call(
        project_kernel,
        out_shape=jax.ShapeDtypeStruct((height, width), BF),
        in_specs=[vmem, vmem],
        out_specs=pl.BlockSpec(memory_space=pltpu.HBM),
        scratch_shapes=[
            pltpu.VMEM((height, depth), BF),
            pltpu.VMEM((width // block, height, block), BF),
            pltpu.SemaphoreType.DMA((width // block,)),
        ],
        compiler_params=pltpu.CompilerParams(vmem_limit_bytes=32 * 2**20),
        name="project",
    )(lhs, weight)


def shards(n, nz, gate_inner, values, gate_outer, filters, skip_bias, out_weight):
    parts = max(1, min(4, gate_inner.shape[0] // n // 2))
    lhs, weight = regroup(
        n, nz, parts, gate_inner, values, gate_outer, filters, skip_bias, out_weight
    )
    return project(lhs, weight)


def solution(mesh):
    n, nz = mesh.shape["seq"], mesh.shape["ch"]
    in_specs = (P("ch", "seq"), P("ch", "seq"), P("ch", "seq"), P("ch", "seq"), P("ch"), P())
    out_specs = P(("seq", "ch"), None)
    return jax.shard_map(
        functools.partial(shards, n, nz),
        mesh=mesh, in_specs=in_specs, out_specs=out_specs, check_vma=False,
    )
```
